512 devices in a mesh: group: 2 (over core), ctx: 32 (over z, x_lo), tp: 8 (over y, x_hi).
Axes of the slice: x: 4 (x_hi: 2, x_lo: 2; x = x_hi * 2 + x_lo), y: 4, z: 16, core: 2. Of those that a mesh axis runs over, the one named last changes fastest.
Arguments:
- normed_hidden_rows: bfloat16 [8192, 8192], P(('group', 'ctx'), 'tp'), may hold values from -6 to 6
- queries: bfloat16 [8192, 8, 1024], P(('group', 'ctx'), 'tp'), may hold values from -500 to 500, as said below
- base_key_value: bfloat16 [8192, 8, 256], P(('group', 'ctx'), 'tp'), may hold values from -6 to 6
- row_adapter_index: int32 [8192], P(('group', 'ctx')), may hold values from 0 to 3
- adapter_down_weight: bfloat16 [8192, 512], P('tp'), may hold values from -0.0625 to 0.0625
- adapter_up_weight: bfloat16 [4, 2, 64, 8, 128], P(None, None, None, 'tp'), may hold values from -0.75 to 0.75
- key_value_cache: bfloat16 [1024, 128, 8, 256], P('ctx', None, 'tp'), may hold values from -6 to 6
- live_cache_length: int32 [1024], P('ctx'), may hold values from 1 to 128, as said below
- receiving_device: int32 [4096, 1], P('ctx'), may hold values from 0 to 31, as said below
- receiving_sequence: int32 [4096], P('ctx'), may hold values from 0 to 31, as said below
Outputs:
- attended: bfloat16 [8192, 8, 1024], P(('group', 'ctx'), 'tp')
The draws below stay inside these ranges and needn't reach their ends.
Inputs may be any that keep to these rules, and one draw needn't show every extreme that they name: Large-magnitude queries occur. `live_cache_length`: lengths differ strongly from decode device to decode device; some sequence has exactly 128 live positions. `receiving_device`: prompt rows come in aligned pages of 8 consecutive rows; all rows of a page name one decode device, and the pages among the rows of one device name different decode devices. `receiving_sequence`: all rows of an aligned page of 8 consecutive rows name one sequence.
All inputs are finite; a program needn't handle non-finite values.
Results may differ from the reference program's by a relative error of at most 0.04.
Values may be sent and summed in bfloat16 or wider, within the bound.
A program may use at most 64 MiB of HBM per device.

```python
import math
import jax
import jax.numpy as jnp
from jax import lax

MODEL_WIDTH = 8192
KEY_VALUE_HEADS = 8
QPK = 8
HEAD_SIZE = 128
ADAPTER_RANK = 64
ADAPTER_COUNT = 4
TOK_DEV = 128
CACHE = 128
SEQ_DEV = 32
CAP = 8
TOKENS = 4096
ALLROWS = 8192
SEQS = 1024
N_CTX = 32


def boosted(booster_key, values):
    strong = jax.random.randint(booster_key, (ALLROWS, 1, 1), 0, 64)
    booster = jnp.where(strong == 0, 20.0, jnp.where(strong == 1, 40.0, jnp.where(strong == 2, 80.0, 1.0)))
    return values * booster


def draw_queries(key, part):
    key = jax.random.fold_in(key, 11)
    first_key = jax.random.fold_in(key, 0)
    third_key = jax.random.fold_in(key, 2)
    full_shape = (ALLROWS, KEY_VALUE_HEADS, QPK * HEAD_SIZE)
    values = boosted(third_key, jnp.clip(jax.random.normal(first_key, full_shape, jnp.float32), -6.0, 6.0))
    return jnp.clip(values, -500.0, 500.0).astype(jnp.bfloat16)


def draw_live_cache_length(key, part):
    key = jax.random.fold_in(key, 23)
    first_key, second_key = jax.random.split(key, 2)
    ranking = jax.random.permutation(first_key, N_CTX)
    heavy = ranking < max(1, N_CTX // 4)
    upper = jnp.where(heavy, CACHE, max(1, CACHE // 4)).astype(jnp.int32)
    seq_upper = jnp.repeat(upper, SEQ_DEV)
    seq_heavy = jnp.repeat(heavy, SEQ_DEV)
    lengths = jax.random.randint(second_key, (SEQS,), 1, seq_upper + 1)
    leading = jnp.arange(SEQS, dtype=jnp.int32) % SEQ_DEV == 0
    lengths = jnp.where(jnp.logical_and(leading, seq_heavy), CACHE, lengths)
    return lengths.astype(jnp.int32)


def page_order(block_key):
    return jax.random.permutation(block_key, N_CTX)


def draw_receiving_device(key, part):
    key = jax.random.fold_in(key, 31)
    pages = TOK_DEV // CAP
    block_keys = jax.random.split(key, N_CTX)
    orders = jax.vmap(page_order)(block_keys)[:, :pages]
    return jnp.repeat(orders.reshape(-1), CAP).reshape(TOKENS, 1).astype(jnp.int32)


def draw_receiving_sequence(key, part):
    key = jax.random.fold_in(key, 37)
    pages = TOK_DEV // CAP
    slots = jax.random.randint(key, (N_CTX * pages,), 0, SEQ_DEV)
    return jnp.repeat(slots, CAP).astype(jnp.int32)


def touch_ends(drawn, own_key, low, high):
    shape = drawn.shape
    spot = [jax.random.randint(jax.random.fold_in(own_key, axis), (), 0, shape[axis]) for axis in range(len(shape))]
    drawn = drawn.at[tuple(spot)].set(low)
    longest = shape.index(max(shape))
    spot[longest] = (spot[longest] + 1) % shape[longest]
    return drawn.at[tuple(spot)].set(high)


def shard_levels(stream_key, shape, pieces, smallest, high):
    loudness, own = 1.0, jax.random.fold_in(stream_key, 6)
    for position, blocks in pieces:
        heights = jnp.exp(jax.random.uniform(jax.random.fold_in(own, position), (blocks,), jnp.float32, smallest / len(pieces), high / len(pieces)))
        loudness = loudness * jnp.repeat(heights, shape[position] // blocks).reshape([-1 if axis == position else 1 for axis in range(len(shape))])
    return loudness


def noise(own_key, shape, deviation, reach, shards=(), held_as=jnp.bfloat16):
    loudness = shard_levels(own_key, shape, shards, -0.22, 0.18) if shards else 1.0
    array = jax.random.normal(own_key, shape, jnp.float32) * deviation * loudness
    return jnp.minimum(jnp.maximum(array, -reach), reach).astype(held_as)


def setup_inputs(seed: int = 0) -> dict:
    key_of = jax.random.split(jax.random.key(seed), 11)
    return {
        "normed_hidden_rows": noise(key_of[0], (ALLROWS, MODEL_WIDTH), 1.0, 6.0, ((0, 64), (1, 8))),
        "queries": draw_queries(jax.random.fold_in(key_of[10], 71), 0),
        "base_key_value": noise(key_of[2], (ALLROWS, KEY_VALUE_HEADS, 2 * HEAD_SIZE), 1.0, 6.0, ((0, 64), (1, 8))),
        "row_adapter_index": touch_ends(jax.random.randint(key_of[3], (ALLROWS,), 0, ADAPTER_COUNT), jax.random.fold_in(key_of[3], 1), 0, ADAPTER_COUNT - 1).astype(jnp.int32),
        "adapter_down_weight": noise(key_of[4], (MODEL_WIDTH, ADAPTER_COUNT * 2 * ADAPTER_RANK), MODEL_WIDTH ** -0.5, 0.0625, ((0, 8),)),
        "adapter_up_weight": noise(key_of[5], (ADAPTER_COUNT, 2, ADAPTER_RANK, KEY_VALUE_HEADS, HEAD_SIZE), ADAPTER_RANK ** -0.5, 0.75, ((3, 8),)),
        "key_value_cache": noise(key_of[6], (SEQS, CACHE, KEY_VALUE_HEADS, 2 * HEAD_SIZE), 1.0, 6.0, ((0, 32), (2, 8))),
        "live_cache_length": draw_live_cache_length(jax.random.fold_in(key_of[10], 71), 0),
        "receiving_device": draw_receiving_device(jax.random.fold_in(key_of[10], 71), 0),
        "receiving_sequence": draw_receiving_sequence(jax.random.fold_in(key_of[10], 71), 0),
    }


def compute_key_projection(normed_hidden_rows, row_adapter_index, base_key_value, adapter_down_weight, adapter_up_weight):
    total_row_count = normed_hidden_rows.shape[0]
    rank_reduced = jnp.dot(normed_hidden_rows, adapter_down_weight, preferred_element_type=jnp.float32).astype(jnp.bfloat16)
    rank_reduced = rank_reduced.reshape(total_row_count, ADAPTER_COUNT, 2, ADAPTER_RANK)
    adapter_selector = row_adapter_index[:, None] == jnp.arange(ADAPTER_COUNT, dtype=jnp.int32)[None, :]
    gathered_adapter = jnp.where(adapter_selector[:, :, None, None], rank_reduced, jnp.zeros((), jnp.bfloat16))
    key_correction = jnp.dot(gathered_adapter[:, :, 0, :].reshape(total_row_count, ADAPTER_COUNT * ADAPTER_RANK), adapter_up_weight[:, 0].reshape(ADAPTER_COUNT * ADAPTER_RANK, KEY_VALUE_HEADS * HEAD_SIZE), preferred_element_type=jnp.float32)
    value_correction = jnp.dot(gathered_adapter[:, :, 1, :].reshape(total_row_count, ADAPTER_COUNT * ADAPTER_RANK), adapter_up_weight[:, 1].reshape(ADAPTER_COUNT * ADAPTER_RANK, KEY_VALUE_HEADS * HEAD_SIZE), preferred_element_type=jnp.float32)
    delta = jnp.concatenate([key_correction.reshape(total_row_count, KEY_VALUE_HEADS, HEAD_SIZE), value_correction.reshape(total_row_count, KEY_VALUE_HEADS, HEAD_SIZE)], axis=2)
    return (base_key_value.astype(jnp.float32) + delta).astype(jnp.bfloat16)

def rounded_weights(weights):
    return lax.optimization_barrier(weights.astype(jnp.bfloat16)).astype(jnp.float32)

def prefill_attention(queries, projected_key_value):
    inv_root = 1.0 / math.sqrt(HEAD_SIZE)
    query_blocks = queries.reshape(N_CTX, TOK_DEV, KEY_VALUE_HEADS, QPK, HEAD_SIZE)
    key_rows = projected_key_value[:, :, :HEAD_SIZE].astype(jnp.float32)
    value_rows = projected_key_value[:, :, HEAD_SIZE:].astype(jnp.float32)
    key_pos = jnp.arange(TOKENS, dtype=jnp.int32)

    def one_block(block_index):
        q_block = lax.dynamic_index_in_dim(query_blocks, block_index, 0, keepdims=False).astype(jnp.float32)
        scores = jnp.einsum('tgqd,sgd->tgqs', q_block, key_rows, precision=lax.Precision.HIGHEST) * inv_root
        query_pos = block_index * TOK_DEV + jnp.arange(TOK_DEV, dtype=jnp.int32)
        allowed = (key_pos[None, :] <= query_pos[:, None])[:, None, None, :]
        scores = jnp.where(allowed, scores, -1e+30)
        peak = lax.optimization_barrier(jnp.max(scores, axis=-1, keepdims=True))
        expos = jnp.where(allowed, jnp.exp(scores - peak), 0.0)
        weights = rounded_weights(expos / lax.optimization_barrier(jnp.sum(expos, axis=-1, keepdims=True)))
        return jnp.einsum('tgqs,sgd->tgqd', weights, value_rows, precision=lax.Precision.HIGHEST)
    outputs = lax.map(one_block, jnp.arange(N_CTX, dtype=jnp.int32))
    return outputs.reshape(TOKENS, KEY_VALUE_HEADS, QPK * HEAD_SIZE)

def decode_block(queries, fresh, cache_rows, seq_lengths, handed, handed_seq):
    key_value_head_count = fresh.shape[1]
    seq_count = seq_lengths.shape[0]
    step_count = fresh.shape[0] // seq_count
    per_head = queries.shape[2] // HEAD_SIZE
    positions = cache_rows.shape[1]
    inv_root = 1.0 / math.sqrt(HEAD_SIZE)
    grouped = queries.reshape(seq_count, step_count, key_value_head_count, per_head, HEAD_SIZE).astype(jnp.float32)
    fresh_rows = fresh.reshape(seq_count, step_count, key_value_head_count, 2 * HEAD_SIZE).astype(jnp.float32)
    cache_f = cache_rows.astype(jnp.float32)
    handed_f = handed.astype(jnp.float32)
    high = lax.Precision.HIGHEST
    cache_scores = jnp.einsum('nkgqd,npgd->nkgqp', grouped, cache_f[..., :HEAD_SIZE], precision=high)
    hand_scores = jnp.einsum('nkgqd,mgd->nkgqm', grouped, handed_f[..., :HEAD_SIZE], precision=high)
    fresh_scores = jnp.einsum('nkgqd,njgd->nkgqj', grouped, fresh_rows[..., :HEAD_SIZE], precision=high)
    scores = jnp.concatenate([cache_scores, hand_scores, fresh_scores], axis=-1) * inv_root
    seq_index = jnp.arange(seq_count, dtype=jnp.int32)
    step_index = jnp.arange(step_count, dtype=jnp.int32)
    cache_ok = jnp.arange(positions, dtype=jnp.int32)[None, :] < seq_lengths[:, None]
    hand_ok = handed_seq[None, :] == seq_index[:, None]
    fresh_ok = step_index[None, :] <= step_index[:, None]
    lead = (seq_count, step_count, key_value_head_count, per_head)
    allowed = jnp.concatenate([jnp.broadcast_to(cache_ok[:, None, None, None, :], lead + (positions,)), jnp.broadcast_to(hand_ok[:, None, None, None, :], lead + (handed.shape[0],)), jnp.broadcast_to(fresh_ok[None, :, None, None, :], lead + (step_count,))], axis=-1)
    scores = jnp.where(allowed, scores, -1e+30)
    peak = lax.optimization_barrier(jnp.max(scores, axis=-1, keepdims=True))
    expos = jnp.where(allowed, jnp.exp(scores - peak), 0.0)
    weights = rounded_weights(expos / lax.optimization_barrier(jnp.sum(expos, axis=-1, keepdims=True)))
    split_hand = positions + handed.shape[0]
    result = jnp.einsum('nkgqp,npgd->nkgqd', weights[..., :positions], cache_f[..., HEAD_SIZE:], precision=high)
    result = result + jnp.einsum('nkgqm,mgd->nkgqd', weights[..., positions:split_hand], handed_f[..., HEAD_SIZE:], precision=high)
    result = result + jnp.einsum('nkgqj,njgd->nkgqd', weights[..., split_hand:], fresh_rows[..., HEAD_SIZE:], precision=high)
    return result.reshape(seq_count * step_count, key_value_head_count, per_head * HEAD_SIZE)

def decode_attention(dec_queries, dec_kv, prompt_kv, key_value_cache, live_cache_length, receiving_device, receiving_sequence):
    capacity = max(2, 2 * TOK_DEV // N_CTX)
    handed_rows = N_CTX * capacity
    owners = receiving_device[:, 0]
    by_owner = jnp.argsort(owners, stable=True)
    sorted_kv = jnp.concatenate([prompt_kv[by_owner], jnp.zeros((handed_rows, KEY_VALUE_HEADS, 2 * HEAD_SIZE), jnp.bfloat16)], axis=0)
    sorted_dev = jnp.concatenate([owners[by_owner], jnp.full((handed_rows,), -1, jnp.int32)], axis=0)
    sorted_slot = jnp.concatenate([receiving_sequence[by_owner], jnp.zeros((handed_rows,), jnp.int32)], axis=0)

    def one_device(device):
        first_row = jnp.sum((owners < device).astype(jnp.int32)).astype(jnp.int32)
        handed = lax.dynamic_slice_in_dim(sorted_kv, first_row, handed_rows, 0)
        hand_dev = lax.dynamic_slice_in_dim(sorted_dev, first_row, handed_rows, 0)
        hand_slot = lax.dynamic_slice_in_dim(sorted_slot, first_row, handed_rows, 0)
        handed_seq = jnp.where(hand_dev == device, hand_slot, -1).astype(jnp.int32)
        row_first = (device * TOK_DEV).astype(jnp.int32)
        seq_first = (device * SEQ_DEV).astype(jnp.int32)
        own_queries = lax.dynamic_slice_in_dim(dec_queries, row_first, TOK_DEV, 0)
        own_fresh = lax.dynamic_slice_in_dim(dec_kv, row_first, TOK_DEV, 0)
        own_cache = lax.dynamic_slice_in_dim(key_value_cache, seq_first, SEQ_DEV, 0)
        own_lengths = lax.dynamic_slice_in_dim(live_cache_length, seq_first, SEQ_DEV, 0)
        return decode_block(own_queries, own_fresh, own_cache, own_lengths, handed, handed_seq)
    outputs = lax.map(one_device, jnp.arange(N_CTX, dtype=jnp.int32))
    return outputs.reshape(TOKENS, KEY_VALUE_HEADS, QPK * HEAD_SIZE)

def reference(normed_hidden_rows, queries, base_key_value, row_adapter_index, adapter_down_weight, adapter_up_weight, key_value_cache, live_cache_length, receiving_device, receiving_sequence):
    projected_key_value = compute_key_projection(normed_hidden_rows, row_adapter_index, base_key_value, adapter_down_weight, adapter_up_weight)
    prompt_out = prefill_attention(queries[:TOKENS], projected_key_value[:TOKENS])
    decode_out = decode_attention(queries[TOKENS:], projected_key_value[TOKENS:], projected_key_value[:TOKENS], key_value_cache, live_cache_length, receiving_device, receiving_sequence)
    return jnp.concatenate([prompt_out, decode_out], axis=0).astype(jnp.bfloat16)
```

```python
import math

import jax
import jax.numpy as jnp
from jax import lax
from jax.experimental import pallas as pl
from jax.experimental.pallas import tpu as pltpu
from jax.sharding import PartitionSpec as P

MESH = pl.DeviceIdType.MESH
ROWS = 128
HEADS = 8
HEAD = 128
RANK2 = 128
ADAPTERS = 4
SEQ_DEV = 32
CACHE = 128
IDROWS = 16
BLOCK = ROWS + IDROWS
NZ = 16
NTP = 8
QROWS = ROWS * HEADS
GROUPS = 8
NEG = -1e30
SCALE = math.log2(math.e) / math.sqrt(HEAD)

OWN_SENDS = [(0, 4, 4), (0, -4, 12), (0, 2, 2), (0, -2, 14), (0, 1, 1), (0, -1, 15)]
FORWARDS = {
    4: [(4, 4, 8), (4, 2, 6), (4, 1, 5)],
    12: [(12, -2, 10), (12, -1, 11)],
    2: [(2, 1, 3)],
    14: [(14, -1, 13)],
    6: [(6, 1, 7)],
    10: [(10, -1, 9)],
}
ALL_SENDS = OWN_SENDS + [s for v in FORWARDS.values() for s in v]
Z_SEM = {send[2]: i for i, send in enumerate(ALL_SENDS)}
X_SEM0 = len(ALL_SENDS)
CORE_SEM0 = X_SEM0 + NZ
SEND_SEMS = CORE_SEM0 + 2 * NZ

PROMPT_PLAN = [
    ("own", 1), ("own", 15), ("own", 2), ("own", 14), ("pair", 0),
    ("own", 4), ("own", 12), ("own", 3), ("own", 13),
    ("pair", 1), ("pair", 15), ("own", 5), ("own", 11), ("pair", 2), ("pair", 14),
    ("own", 6), ("own", 10), ("pair", 4), ("pair", 12),
    ("own", 8), ("pair", 3), ("pair", 13), ("own", 7), ("own", 9),
    ("pair", 5), ("pair", 11), ("pair", 6), ("pair", 10), ("pair", 8), ("pair", 7), ("pair", 9),
]
DECODE_PLAN = [0, 1, 15, 2, 14, 4, 12, 3, 13, 5, 11, 6, 10, 8, 7, 9]


def kernel(
    hid_ref, q_ref, base_ref, idx_ref, down_ref, up_ref, cache_ref, len_ref, rd_ref, rs_ref,
    out_ref,
    hid, qin, base, idx, down, up, cache, lens, rd, rs,
    part, landed, kv, fresh, q, top, acc, tot, wide,
    load_sem, tp_send, tp_recv, kv_send, kv_recv,
):
    group = lax.axis_index("group")
    ctx = lax.axis_index("ctx")
    tp = lax.axis_index("tp")
    z = ctx // 2
    x_lo = ctx % 2

    def z_peer(step):
        return {"ctx": lax.rem(z + step + NZ, NZ) * 2 + x_lo}

    x_peer = {"ctx": z * 2 + (1 - x_lo)}
    core_peer = {"group": 1 - group}

    barrier = pltpu.get_barrier_semaphore()
    peers = [{"tp": lax.rem(tp + d, NTP)} for d in range(1, NTP)]
    peers += [z_peer(s) for s in (4, -4, 2, -2, 1, -1)]
    peers += [x_peer, core_peer]
    for peer in peers:
        pl.semaphore_signal(barrier, inc=1, device_id=peer, device_id_type=MESH)

    loads = [
        pltpu.make_async_copy(src, dst, load_sem.at[i])
        for i, (src, dst) in enumerate(
            [(hid_ref, hid), (down_ref, down), (idx_ref, idx), (up_ref, up), (base_ref, base),
             (rd_ref, rd), (rs_ref, rs), (q_ref, qin), (len_ref, lens), (cache_ref, cache)]
        )
    ]
    for load in loads[:9]:
        load.start()

    @pl.when(group == 1)
    def _():
        loads[9].start()

    for load in loads[:3]:
        load.wait()

    eye = lax.broadcasted_iota(jnp.int32, (ROWS, ROWS), 0) == lax.broadcasted_iota(
        jnp.int32, (ROWS, ROWS), 1
    )
    adapter = jnp.sum(
        jnp.where(eye, jnp.broadcast_to(idx[...].astype(jnp.float32), (ROWS, ROWS)), 0.0),
        axis=1,
        keepdims=True,
    )
    shrunk = jnp.dot(hid[...], down[...], preferred_element_type=jnp.float32)
    picked = jnp.zeros((ROWS, RANK2), jnp.float32)
    for a in range(ADAPTERS):
        picked = jnp.where(adapter == float(a), shrunk[:, a * RANK2 : (a + 1) * RANK2], picked)
    part[...] = picked
    pl.semaphore_wait(barrier, len(peers))

    tp_copies = [
        pltpu.make_async_remote_copy(
            src_ref=part,
            dst_ref=landed.at[d],
            send_sem=tp_send.at[d],
            recv_sem=tp_recv.at[d],
            device_id={"tp": lax.rem(tp + d, NTP)},
            device_id_type=MESH,
        )
        for d in range(1, NTP)
    ]
    for d in (3, 5, 4, 7, 1, 6, 2):
        tp_copies[d - 1].start()

    for load in loads[3:9]:
        load.wait()
    for g in range(GROUPS):
        for j in range(HEADS):
            q[g * 128 + j * 16 : g * 128 + (j + 1) * 16, :] = qin[
                g * 16 : (g + 1) * 16, j * HEAD : (j + 1) * HEAD
            ]
    is_key = (lax.broadcasted_iota(jnp.int32, (ADAPTERS * RANK2, HEAD), 0) // 64) % 2 == 0
    zero = jnp.zeros((), jnp.float32)
    up_f = up[...].astype(jnp.float32)
    wide[:, :HEAD] = jnp.where(is_key, up_f, zero).astype(jnp.bfloat16)
    wide[:, HEAD:] = jnp.where(is_key, zero, up_f).astype(jnp.bfloat16)

    def scores_of(queries, keys):
        return lax.dot_general(
            queries, keys, (((1,), (1,)), ((), ())), preferred_element_type=jnp.float32
        )

    def weighted(weights, values):
        ones = jnp.ones(values.shape, jnp.bfloat16)
        return jnp.dot(
            weights.astype(jnp.bfloat16),
            jnp.concatenate([values, ones], axis=1),
            preferred_element_type=jnp.float32,
        )

    def first_keys(rows, scores, values):
        peak = jnp.max(scores, axis=1, keepdims=True)
        both = weighted(jnp.exp2((scores - peak) * SCALE), values)
        top[rows, :] = jnp.broadcast_to(peak, (peak.shape[0], HEAD))
        acc[rows, :] = both[:, :HEAD]
        tot[rows, :] = both[:, HEAD:]

    def more_keys(rows, scores, values):
        before = top[rows, :]
        after = jnp.maximum(before, jnp.max(scores, axis=1, keepdims=True))
        rescale = jnp.exp2((before - after) * SCALE)
        both = weighted(jnp.exp2((scores - after[:, :1]) * SCALE), values)
        top[rows, :] = after
        acc[rows, :] = acc[rows, :] * rescale + both[:, :HEAD]
        tot[rows, :] = tot[rows, :] * rescale + both[:, HEAD:]

    def row_token(first, count):
        row = lax.broadcasted_iota(jnp.int32, (count, 1), 0) + first
        return (row // 128) * 16 + row % 16

    STEP = 256

    def by_rows(body):
        def one(i, carry):
            first = pl.multiple_of(i * STEP, STEP)
            body(pl.ds(first, STEP), first)
            return carry

        lax.fori_loop(0, QROWS // STEP, one, 0)

    @pl.when(group == 1)
    def _():
        loads[9].wait()
        column = lax.broadcasted_iota(jnp.int32, (1, CACHE), 1)
        for g in range(GROUPS):
            rows = pl.ds(g * 128, 128)
            block = cache[4 * g : 4 * g + 4].reshape(4 * CACHE, 2 * HEAD)
            scores = scores_of(q[rows, :], block[:, :HEAD])
            own = (lax.broadcasted_iota(jnp.int32, (128, 1), 0) % 16) // 4
            pieces = []
            for n in range(4):
                ok = jnp.logical_and(own == n, column < lens[4 * g + n])
                pieces.append(jnp.where(ok, scores[:, n * CACHE : (n + 1) * CACHE], NEG))
            first_keys(rows, jnp.concatenate(pieces, axis=1), block[:, HEAD:])

    for copy in tp_copies:
        copy.wait_recv()
    total = picked
    for d in range(1, NTP):
        total = total + landed[d]
    spread = jnp.concatenate(
        [
            jnp.where(adapter == float(a), total, 0.0).astype(jnp.bfloat16)
            for a in range(ADAPTERS)
        ],
        axis=1,
    )
    delta = jnp.dot(spread, wide[...], preferred_element_type=jnp.float32)
    own_kv = (base[...].astype(jnp.float32) + delta).astype(jnp.bfloat16)

    def z_copy(source, step, dest):
        i = Z_SEM[dest]
        return pltpu.make_async_remote_copy(
            src_ref=kv.at[source, 0], dst_ref=kv.at[dest, 0],
            send_sem=kv_send.at[i], recv_sem=kv_recv.at[2 * dest],
            device_id=z_peer(step), device_id_type=MESH,
        )

    def x_copy(slot):
        return pltpu.make_async_remote_copy(
            src_ref=kv.at[slot, 0], dst_ref=kv.at[slot, 1],
            send_sem=kv_send.at[X_SEM0 + slot], recv_sem=kv_recv.at[2 * slot + 1],
            device_id=x_peer, device_id_type=MESH,
        )

    def core_copy(slot, side):
        return pltpu.make_async_remote_copy(
            src_ref=kv.at[slot, side], dst_ref=kv.at[slot, side],
            send_sem=kv_send.at[CORE_SEM0 + 2 * slot + side],
            recv_sem=kv_recv.at[2 * slot + side],
            device_id=core_peer, device_id_type=MESH,
        )

    def pair_of(slot):
        keys = jnp.concatenate([kv[slot, 0, :ROWS, :HEAD], kv[slot, 1, :ROWS, :HEAD]], axis=0)
        values = jnp.concatenate([kv[slot, 0, :ROWS, HEAD:], kv[slot, 1, :ROWS, HEAD:]], axis=0)
        return keys, values

    @pl.when(group == 0)
    def _():
        kv[0, 0, :ROWS, :] = own_kv
        ids = jnp.concatenate([rd[...], rs[...]], axis=1).astype(jnp.float32)
        kv[0, 0, ROWS:, :] = jnp.broadcast_to(ids, (IDROWS, 2 * HEAD)).astype(jnp.bfloat16)
        for send in OWN_SENDS:
            z_copy(*send).start()
        x_copy(0).start()
        core_copy(0, 0).start()

        def diagonal(rows, first):
            token = row_token(first, STEP)
            ok = lax.broadcasted_iota(jnp.int32, (1, ROWS), 1) <= token
            scores = jnp.where(ok, scores_of(q[rows, :], kv[0, 0, :ROWS, :HEAD]), NEG)
            first_keys(rows, scores, kv[0, 0, :ROWS, HEAD:])

        by_rows(diagonal)
        for what, slot in PROMPT_PLAN:
            if what == "own":
                z_copy(0, 1, slot).wait_recv()
                for send in FORWARDS.get(slot, []):
                    z_copy(*send).start()
                x_copy(slot).start()
                core_copy(slot, 0).start()
            else:
                x_copy(slot).wait_recv()
                core_copy(slot, 1).start()
                if slot == 0:

                    @pl.when(x_lo == 1)
                    def _():
                        def side(rows, first):
                            more_keys(
                                rows,
                                scores_of(q[rows, :], kv[0, 1, :ROWS, :HEAD]),
                                kv[0, 1, :ROWS, HEAD:],
                            )

                        by_rows(side)
                else:

                    @pl.when(z >= slot)
                    def _():
                        keys, values = pair_of(slot)

                        def both(rows, first):
                            more_keys(rows, scores_of(q[rows, :], keys), values)

                        by_rows(both)

    @pl.when(group == 1)
    def _():
        fresh[...] = own_kv
        me = ctx.astype(jnp.float32)

        def steps(rows, first):
            token = row_token(first, STEP)
            column = lax.broadcasted_iota(jnp.int32, (1, ROWS), 1)
            ok = jnp.logical_and(column // 4 == token // 4, column <= token)
            scores = jnp.where(ok, scores_of(q[rows, :], fresh[:, :HEAD]), NEG)
            more_keys(rows, scores, fresh[:, HEAD:])

        by_rows(steps)
        for slot in DECODE_PLAN:
            for side in (0, 1):
                core_copy(slot, side).wait_recv()
            keys, values = pair_of(slot)
            ids = jnp.concatenate(
                [kv[slot, 0, ROWS:, :], kv[slot, 1, ROWS:, :]], axis=0
            ).astype(jnp.float32)
            device = jnp.concatenate([ids[:1, :HEAD], ids[IDROWS : IDROWS + 1, :HEAD]], axis=1)
            sequence = jnp.concatenate([ids[:1, HEAD:], ids[IDROWS : IDROWS + 1, HEAD:]], axis=1)
            code = jnp.where(device == me, sequence, -1.0)

            def handed(rows, first):
                own = (row_token(first, STEP) // 4).astype(jnp.float32)
                scores = jnp.where(code == own, scores_of(q[rows, :], keys), NEG)
                more_keys(rows, scores, values)

            by_rows(handed)

    for g in range(GROUPS):
        rows = pl.ds(g * 128, 128)
        result = (acc[rows, :] / tot[rows, :]).astype(jnp.bfloat16)
        for j in range(HEADS):
            out_ref[g * 16 : (g + 1) * 16, j * HEAD : (j + 1) * HEAD] = result[
                j * 16 : (j + 1) * 16
            ]

    for copy in tp_copies:
        copy.wait_send()

    @pl.when(group == 0)
    def _():
        for send in ALL_SENDS:
            z_copy(*send).wait_send()
        for slot in range(NZ):
            x_copy(slot).wait_send()
            core_copy(slot, 0).wait_send()
            core_copy(slot, 1).wait_send()


def body(hidden, queries, base, adapter, down, up, cache, lengths, device, sequence):
    vmem = pltpu.VMEM
    bf16, f32, i32 = jnp.bfloat16, jnp.float32, jnp.int32
    out = pl.pallas_call(
        kernel,
        out_shape=jax.ShapeDtypeStruct((ROWS, HEADS * HEAD), bf16),
        in_specs=[pl.BlockSpec(memory_space=pl.ANY)] * 10,
        out_specs=pl.BlockSpec(memory_space=vmem),
        scratch_shapes=[
            vmem((ROWS, 1024), bf16),
            vmem((ROWS, HEADS * HEAD), bf16),
            vmem((ROWS, 2 * HEAD), bf16),
            vmem((1, ROWS), i32),
            vmem((1024, ADAPTERS * RANK2), bf16),
            vmem((ADAPTERS * RANK2, HEAD), bf16),
            vmem((SEQ_DEV, CACHE, 2 * HEAD), bf16),
            pltpu.SMEM((SEQ_DEV,), i32),
            vmem((1, ROWS), i32),
            vmem((1, ROWS), i32),
            vmem((ROWS, RANK2), f32),
            vmem((NTP, ROWS, RANK2), f32),
            vmem((NZ, 2, BLOCK, 2 * HEAD), bf16),
            vmem((ROWS, 2 * HEAD), bf16),
            vmem((QROWS, HEAD), bf16),
            vmem((QROWS, HEAD), f32),
            vmem((QROWS, HEAD), f32),
            vmem((QROWS, HEAD), f32),
            vmem((ADAPTERS * RANK2, 2 * HEAD), bf16),
            pltpu.SemaphoreType.DMA((10,)),
            pltpu.SemaphoreType.DMA((NTP,)),
            pltpu.SemaphoreType.DMA((NTP,)),
            pltpu.SemaphoreType.DMA((SEND_SEMS,)),
            pltpu.SemaphoreType.DMA((2 * NZ,)),
        ],
        compiler_params=pltpu.CompilerParams(
            collective_id=0, has_side_effects=True, vmem_limit_bytes=60 << 20
        ),
        name="attention",
    )(
        hidden,
        queries.reshape(ROWS, HEADS * HEAD),
        base.reshape(ROWS, 2 * HEAD),
        adapter.reshape(1, ROWS),
        down,
        up.reshape(ADAPTERS * RANK2, HEAD),
        cache.reshape(SEQ_DEV, CACHE, 2 * HEAD),
        lengths,
        device.reshape(1, ROWS),
        sequence.reshape(1, ROWS),
    )
    return out.reshape(ROWS, 1, HEADS * HEAD)


def solution(mesh):
    return jax.shard_map(
        body,
        mesh=mesh,
        in_specs=(
            P(("group", "ctx"), "tp"),
            P(("group", "ctx"), "tp", None),
            P(("group", "ctx"), "tp", None),
            P(("group", "ctx")),
            P("tp", None),
            P(None, None, None, "tp", None),
            P("ctx", None, "tp", None),
            P("ctx"),
            P("ctx", None),
            P("ctx"),
        ),
        out_specs=P(("group", "ctx"), "tp", None),
        check_vma=False,
    )
```

```python
import math

import jax
import jax.numpy as jnp
from jax import lax
from jax.experimental import pallas as pl
from jax.experimental.pallas import tpu as pltpu
from jax.sharding import PartitionSpec as P

MESH = pl.DeviceIdType.MESH
ROWS = 128
HEADS = 8
HEAD = 128
RANK2 = 128
ADAPTERS = 4
SEQ_DEV = 32
CACHE = 128
IDROWS = 8
NZ = 16
NTP = 8
QROWS = ROWS * HEADS
GROUPS = 8
NEG = -1e30
SCALE = math.log2(math.e) / math.sqrt(HEAD)

ORDER = [0, 1, 15, 3, 13, 2, 14, 4, 12, 6, 10, 5, 11, 7, 9, 8]
PLACE = {slot: i for i, slot in enumerate(ORDER)}
CHUNK = 4
CHUNKS = NZ // CHUNK
KEYS = CHUNK * 2 * ROWS
PAGES = CHUNK * 2 * 8
OWN_SENDS = [(0, 3, 3), (0, -3, 13), (0, 1, 1), (0, -1, 15)]
FORWARDS = {
    3: [(3, 3, 6), (3, 1, 4)],
    13: [(13, -3, 10), (13, -1, 12)],
    1: [(1, 1, 2)],
    15: [(15, -1, 14)],
    4: [(4, 1, 5)],
    12: [(12, -1, 11)],
    6: [(6, 2, 8), (6, 1, 7)],
    10: [(10, -1, 9)],
}
RELAYS = [send for sends in FORWARDS.values() for send in sends]
ARRIVALS = [
    (3, 0), (13, 0), (1, 0), (15, 0), (0, 1), (2, 0), (14, 0), (4, 0), (12, 0), (3, 1), (13, 1),
    (1, 1), (15, 1), (6, 0), (10, 0), (2, 1), (14, 1), (4, 1), (12, 1), (5, 0), (11, 0), (6, 1),
    (10, 1), (7, 0), (9, 0), (8, 0), (5, 1), (11, 1), (7, 1), (9, 1), (8, 1),
]
PARTIAL_ORDER = (3, 5, 4, 7, 1, 6, 2)


def kernel(
    hid_ref, q_ref, base_ref, idx_ref, down_ref, up_ref, cache_ref, len_ref, rd_ref, rs_ref,
    out_ref,
    hid, qin, base, idx, down, up, cache, lens, rd, rs,
    part, landed, kv, ids, fresh, choose, handed, q, top, acc, tot, wide,
    load_sem, tp_send, tp_recv, kv_send, kv_recv, core_send, id_send, id_recv,
):
    group = lax.axis_index("group")
    ctx = lax.axis_index("ctx")
    tp = lax.axis_index("tp")
    z = ctx // 2
    x_lo = ctx % 2

    def at(step, other, core):
        side = 1 - x_lo if other else x_lo
        return {"group": core, "ctx": lax.rem(z + step + NZ, NZ) * 2 + side}

    barrier = pltpu.get_barrier_semaphore()

    def greet(peers):
        for peer in peers:
            pl.semaphore_signal(barrier, inc=1, device_id=peer, device_id_type=MESH)

    tp_peers = [{"tp": lax.rem(tp + d, NTP)} for d in range(1, NTP)]
    greet(tp_peers)

    @pl.when(group == 0)
    def _():
        greet([at(0, False, 1)])

    @pl.when(group == 1)
    def _():
        greet([at(step, False, 0) for step in (3, -3, 1, -1, 0)] + [at(0, True, 0)])
        greet([at(step, False, 1) for step in (3, -3, 2, -2, 1, -1)] + [at(0, True, 1)])

    loads = [
        pltpu.make_async_copy(src, dst, load_sem.at[i])
        for i, (src, dst) in enumerate(
            [(hid_ref, hid), (down_ref, down), (idx_ref, idx), (up_ref, up), (base_ref, base),
             (rd_ref, rd), (rs_ref, rs), (q_ref, qin), (len_ref, lens), (cache_ref, cache)]
        )
    ]
    for load in loads[:9]:
        load.start()

    @pl.when(group == 1)
    def _():
        loads[9].start()

    for load in loads[:3]:
        load.wait()

    eye = lax.broadcasted_iota(jnp.int32, (ROWS, ROWS), 0) == lax.broadcasted_iota(
        jnp.int32, (ROWS, ROWS), 1
    )
    adapter = jnp.sum(
        jnp.where(eye, jnp.broadcast_to(idx[...].astype(jnp.float32), (ROWS, ROWS)), 0.0),
        axis=1,
        keepdims=True,
    )
    shrunk = jnp.dot(hid[...], down[...], preferred_element_type=jnp.float32)
    picked = jnp.zeros((ROWS, RANK2), jnp.float32)
    for a in range(ADAPTERS):
        picked = jnp.where(adapter == float(a), shrunk[:, a * RANK2 : (a + 1) * RANK2], picked)
    part[...] = picked

    @pl.when(group == 0)
    def _():
        pl.semaphore_wait(barrier, 13)

    @pl.when(group == 1)
    def _():
        pl.semaphore_wait(barrier, 15)

    tp_copies = [
        pltpu.make_async_remote_copy(
            src_ref=part, dst_ref=landed.at[d],
            send_sem=tp_send.at[d], recv_sem=tp_recv.at[d],
            device_id=tp_peers[d - 1], device_id_type=MESH,
        )
        for d in range(1, NTP)
    ]

    def id_copy(source, step, dest, side):
        i = 2 * dest + side
        return pltpu.make_async_remote_copy(
            src_ref=ids.at[source, 0], dst_ref=ids.at[dest, side],
            send_sem=id_send.at[i], recv_sem=id_recv.at[i],
            device_id=at(step, side == 1, 1), device_id_type=MESH,
        )

    @pl.when(group == 0)
    def _():
        for d in PARTIAL_ORDER:
            tp_copies[d - 1].start()

    for load in loads[3:9]:
        load.wait()

    @pl.when(group == 1)
    def _():
        ids[0, 0] = jnp.concatenate(
            [rd[...], rs[...], jnp.zeros((IDROWS - 2, ROWS), jnp.int32)], axis=0
        )
        for send in OWN_SENDS:
            id_copy(*send, 0).start()
        id_copy(0, 0, 0, 1).start()

    for g in range(GROUPS):
        for j in range(HEADS):
            q[g * 128 + j * 16 : g * 128 + (j + 1) * 16, :] = qin[
                g * 16 : (g + 1) * 16, j * HEAD : (j + 1) * HEAD
            ]
    is_key = (lax.broadcasted_iota(jnp.int32, (ADAPTERS * RANK2, HEAD), 0) // 64) % 2 == 0
    up_f = up[...].astype(jnp.float32)
    wide[:, :HEAD] = jnp.where(is_key, up_f, 0.0).astype(jnp.bfloat16)
    wide[:, HEAD:] = jnp.where(is_key, 0.0, up_f).astype(jnp.bfloat16)

    def scores_of(queries, keys):
        return lax.dot_general(
            queries, keys, (((1,), (1,)), ((), ())), preferred_element_type=jnp.float32
        )

    def weighted(weights, values):
        ones = jnp.ones(values.shape, jnp.bfloat16)
        return jnp.dot(
            weights.astype(jnp.bfloat16),
            jnp.concatenate([values, ones], axis=1),
            preferred_element_type=jnp.float32,
        )

    def first_keys(rows, scores, values):
        peak = jnp.max(scores, axis=1, keepdims=True)
        both = weighted(jnp.exp2((scores - peak) * SCALE), values)
        top[rows, :] = jnp.broadcast_to(peak, (peak.shape[0], HEAD))
        acc[rows, :] = both[:, :HEAD]
        tot[rows, :] = both[:, HEAD:]

    def more_keys(rows, scores, values):
        before = top[rows, :]
        after = jnp.maximum(before, jnp.max(scores, axis=1, keepdims=True))
        rescale = jnp.exp2((before - after) * SCALE)
        both = weighted(jnp.exp2((scores - after[:, :1]) * SCALE), values)
        top[rows, :] = after
        acc[rows, :] = acc[rows, :] * rescale + both[:, :HEAD]
        tot[rows, :] = tot[rows, :] * rescale + both[:, HEAD:]

    row16 = lax.broadcasted_iota(jnp.int32, (128, 1), 0) % 16

    @pl.when(group == 1)
    def _():
        loads[9].wait()
        column = lax.broadcasted_iota(jnp.int32, (1, CACHE), 1)
        for g in range(GROUPS):
            rows = slice(g * 128, (g + 1) * 128)
            block = cache[4 * g : 4 * g + 4].reshape(4 * CACHE, 2 * HEAD)
            scores = scores_of(q[rows, :], block[:, :HEAD])
            own = row16 // 4
            pieces = []
            for n in range(4):
                ok = jnp.logical_and(own == n, column < lens[4 * g + n])
                pieces.append(jnp.where(ok, scores[:, n * CACHE : (n + 1) * CACHE], NEG))
            first_keys(rows, jnp.concatenate(pieces, axis=1), block[:, HEAD:])

        for d in PARTIAL_ORDER:
            tp_copies[d - 1].start()
        for slot, side in ARRIVALS:
            if side == 0:
                id_copy(0, 1, slot, 0).wait_recv()
                for send in FORWARDS.get(slot, []):
                    id_copy(*send, 0).start()
                id_copy(slot, 0, slot, 1).start()
            else:
                id_copy(slot, 0, slot, 1).wait_recv()
        page = lax.broadcasted_iota(jnp.int32, (PAGES, KEYS), 0)
        key = lax.broadcasted_iota(jnp.int32, (PAGES, KEYS), 1)
        same = jnp.logical_and(page // 8 == key // ROWS, page % 8 == key % 8)
        for c in range(CHUNKS):
            slots = ORDER[c * CHUNK : (c + 1) * CHUNK]
            device = jnp.concatenate([ids[s, d, :1] for s in slots for d in (0, 1)], axis=1)
            mine = jnp.logical_and(same, device == ctx)
            choose[c] = jnp.where(mine, 1.0, 0.0).astype(jnp.bfloat16)

    def own_rows():
        for copy in tp_copies:
            copy.wait_recv()
        total = picked
        for d in range(1, NTP):
            total = total + landed[d]
        spread = jnp.concatenate(
            [
                jnp.where(adapter == float(a), total, 0.0).astype(jnp.bfloat16)
                for a in range(ADAPTERS)
            ],
            axis=1,
        )
        delta = jnp.dot(spread, wide[...], preferred_element_type=jnp.float32)
        return (base[...].astype(jnp.float32) + delta).astype(jnp.bfloat16)

    def kv_copy(source, step, dest, side):
        i = 2 * PLACE[dest] + side
        return pltpu.make_async_remote_copy(
            src_ref=kv.at[PLACE[source], 0], dst_ref=kv.at[PLACE[dest], side],
            send_sem=kv_send.at[i], recv_sem=kv_recv.at[i],
            device_id=at(step, side == 1, 1), device_id_type=MESH,
        )

    def core_copy(slot, side):
        i = 2 * PLACE[slot] + side
        return pltpu.make_async_remote_copy(
            src_ref=kv.at[PLACE[slot], side], dst_ref=kv.at[PLACE[slot], side],
            send_sem=core_send.at[i], recv_sem=kv_recv.at[i],
            device_id={"group": 1 - group}, device_id_type=MESH,
        )

    def chunk_of(c):
        block = kv[c * CHUNK : (c + 1) * CHUNK].reshape(KEYS, 2 * HEAD)
        return block[:, :HEAD], block[:, HEAD:]

    @pl.when(group == 0)
    def _():
        kv[0, 0] = own_rows()
        for send in OWN_SENDS:
            kv_copy(*send, 0).start()
        kv_copy(0, 0, 0, 1).start()
        core_copy(0, 0).start()
        for c in range(CHUNKS):
            slots = ORDER[c * CHUNK : (c + 1) * CHUNK]
            for slot in slots:
                for side in (0, 1):
                    if (slot, side) != (0, 0):
                        core_copy(slot, side).wait_recv()
            limit = [jnp.where(z >= slot, 0.0, NEG) for slot in slots for _ in (0, 1)]
            if c == 0:
                limit[1] = jnp.where(x_lo == 1, 0.0, NEG)

            def chunk(c=c, slots=slots, limit=limit):
                keys, values = chunk_of(c)
                bias = jnp.concatenate(
                    [jnp.full((1, ROWS), value, jnp.float32) for value in limit], axis=1
                )
                for g in range(GROUPS):
                    rows = slice(g * 128, (g + 1) * 128)
                    scores = scores_of(q[rows, :], keys) + bias
                    if c == 0:
                        column = lax.broadcasted_iota(jnp.int32, (1, ROWS), 1)
                        diagonal = jnp.where(column <= g * 16 + row16, scores[:, :ROWS], NEG)
                        scores = jnp.concatenate([diagonal, scores[:, ROWS:]], axis=1)
                        first_keys(rows, scores, values)
                    else:
                        more_keys(rows, scores, values)

            if c == 0:
                chunk()
            else:
                pl.when(z >= min(slots))(chunk)

    @pl.when(group == 1)
    def _():
        seen = set()
        core_copy(0, 0).wait_recv()
        seen.add((0, 0))
        ready = 0
        for slot, side in ARRIVALS:
            if side == 0:
                kv_copy(0, 1, slot, 0).wait_recv()
                for send in FORWARDS.get(slot, []):
                    kv_copy(*send, 0).start()
                kv_copy(slot, 0, slot, 1).start()
            else:
                kv_copy(slot, 0, slot, 1).wait_recv()
            core_copy(slot, side).start()
            seen.add((slot, side))
            if (slot, side) == (12, 1):
                fresh[...] = own_rows()
            slots = ORDER[ready * CHUNK : (ready + 1) * CHUNK]
            if all((s, d) in seen for s in slots for d in (0, 1)):
                block = kv[ready * CHUNK : (ready + 1) * CHUNK].reshape(KEYS, 2 * HEAD)
                handed[ready * PAGES : (ready + 1) * PAGES, :] = jnp.dot(
                    choose[ready], block, preferred_element_type=jnp.float32
                ).astype(jnp.bfloat16)
                ready += 1
        assert ready == CHUNKS
        codes = []
        for c in range(CHUNKS):
            slots = ORDER[c * CHUNK : (c + 1) * CHUNK]
            sequence = jnp.concatenate([ids[s, d, 1:2] for s in slots for d in (0, 1)], axis=1)
            sequence = jnp.broadcast_to(sequence.astype(jnp.float32) + 1.0, (16, KEYS))
            codes.append(scores_of(sequence.astype(jnp.bfloat16), choose[c])[:1])
        code = jnp.concatenate(codes, axis=1) - 1.0
        both = jnp.concatenate([handed[...], fresh[...]], axis=0)
        column = lax.broadcasted_iota(jnp.int32, (1, ROWS), 1)
        for g in range(GROUPS):
            rows = slice(g * 128, (g + 1) * 128)
            token = g * 16 + row16
            scores = scores_of(q[rows, :], both[:, :HEAD])
            step_ok = jnp.logical_and(column // 4 == token // 4, column <= token)
            handed_ok = code == (token // 4).astype(jnp.float32)
            scores = jnp.concatenate(
                [
                    jnp.where(handed_ok, scores[:, : CHUNKS * PAGES], NEG),
                    jnp.where(step_ok, scores[:, CHUNKS * PAGES :], NEG),
                ],
                axis=1,
            )
            more_keys(rows, scores, both[:, HEAD:])

    for g in range(GROUPS):
        rows = slice(g * 128, (g + 1) * 128)
        result = (acc[rows, :] / tot[rows, :]).astype(jnp.bfloat16)
        for j in range(HEADS):
            out_ref[g * 16 : (g + 1) * 16, j * HEAD : (j + 1) * HEAD] = result[
                j * 16 : (j + 1) * 16
            ]

    for copy in tp_copies:
        copy.wait_send()

    @pl.when(group == 0)
    def _():
        for send in OWN_SENDS:
            kv_copy(*send, 0).wait_send()
        kv_copy(0, 0, 0, 1).wait_send()
        core_copy(0, 0).wait_send()

    @pl.when(group == 1)
    def _():
        for send in OWN_SENDS:
            id_copy(*send, 0).wait_send()
        id_copy(0, 0, 0, 1).wait_send()
        for send in RELAYS:
            id_copy(*send, 0).wait_send()
            kv_copy(*send, 0).wait_send()
        for slot, side in ARRIVALS:
            core_copy(slot, side).wait_send()
            if side == 0:
                id_copy(slot, 0, slot, 1).wait_send()
                kv_copy(slot, 0, slot, 1).wait_send()


def body(hidden, queries, base, adapter, down, up, cache, lengths, device, sequence):
    vmem = pltpu.VMEM
    dma = pltpu.SemaphoreType.DMA
    bf16, f32, i32 = jnp.bfloat16, jnp.float32, jnp.int32
    out = pl.pallas_call(
        kernel,
        out_shape=jax.ShapeDtypeStruct((ROWS, HEADS * HEAD), bf16),
        in_specs=[pl.BlockSpec(memory_space=pl.ANY)] * 10,
        out_specs=pl.BlockSpec(memory_space=vmem),
        scratch_shapes=[
            vmem((ROWS, 1024), bf16),
            vmem((ROWS, HEADS * HEAD), bf16),
            vmem((ROWS, 2 * HEAD), bf16),
            vmem((1, ROWS), i32),
            vmem((1024, ADAPTERS * RANK2), bf16),
            vmem((ADAPTERS * RANK2, HEAD), bf16),
            vmem((SEQ_DEV, CACHE, 2 * HEAD), bf16),
            pltpu.SMEM((SEQ_DEV,), i32),
            vmem((1, ROWS), i32),
            vmem((1, ROWS), i32),
            vmem((ROWS, RANK2), f32),
            vmem((NTP, ROWS, RANK2), f32),
            vmem((NZ, 2, ROWS, 2 * HEAD), bf16),
            vmem((NZ, 2, IDROWS, ROWS), i32),
            vmem((ROWS, 2 * HEAD), bf16),
            vmem((CHUNKS, PAGES, KEYS), bf16),
            vmem((CHUNKS * PAGES, 2 * HEAD), bf16),
            vmem((QROWS, HEAD), bf16),
            vmem((QROWS, HEAD), f32),
            vmem((QROWS, HEAD), f32),
            vmem((QROWS, HEAD), f32),
            vmem((ADAPTERS * RANK2, 2 * HEAD), bf16),
            dma((10,)), dma((NTP,)), dma((NTP,)), dma((2 * NZ,)), dma((2 * NZ,)),
            dma((2 * NZ,)), dma((2 * NZ,)), dma((2 * NZ,)),
        ],
        compiler_params=pltpu.CompilerParams(
            collective_id=0, has_side_effects=True, vmem_limit_bytes=60 << 20
        ),
        name="attention",
    )(
        hidden,
        queries.reshape(ROWS, HEADS * HEAD),
        base.reshape(ROWS, 2 * HEAD),
        adapter.reshape(1, ROWS),
        down,
        up.reshape(ADAPTERS * RANK2, HEAD),
        cache.reshape(SEQ_DEV, CACHE, 2 * HEAD),
        lengths,
        device.reshape(1, ROWS),
        sequence.reshape(1, ROWS),
    )
    return out.reshape(ROWS, 1, HEADS * HEAD)


def solution(mesh):
    return jax.shard_map(
        body,
        mesh=mesh,
        in_specs=(
            P(("group", "ctx"), "tp"),
            P(("group", "ctx"), "tp", None),
            P(("group", "ctx"), "tp", None),
            P(("group", "ctx")),
            P("tp", None),
            P(None, None, None, "tp", None),
            P("ctx", None, "tp", None),
            P("ctx"),
            P("ctx", None),
            P("ctx"),
        ),
        out_specs=P(("group", "ctx"), "tp", None),
        check_vma=False,
    )
```

```python
import math

import jax
import jax.numpy as jnp
from jax import lax
from jax.experimental import pallas as pl
from jax.experimental.pallas import tpu as pltpu
from jax.sharding import PartitionSpec as P

MESH = pl.DeviceIdType.MESH
ROWS = 128
HEADS = 8
HEAD = 128
RANK2 = 128
ADAPTERS = 4
SEQ_DEV = 32
CACHE = 128
IDROWS = 8
NZ = 16
NTP = 8
QROWS = ROWS * HEADS
GROUPS = 8
NEG = -1e30
SCALE = math.log2(math.e) / math.sqrt(HEAD)

ORDER = [0, 1, 15, 3, 13, 2, 14, 4, 12, 6, 10, 5, 11, 7, 9, 8]
PLACE = {slot: i for i, slot in enumerate(ORDER)}
CHUNK = 4
CHUNKS = NZ // CHUNK
KEYS = CHUNK * 2 * ROWS
PAGES = CHUNK * 2 * 8
OWN_SENDS = [(0, 3, 3), (0, -3, 13), (0, 1, 1), (0, -1, 15)]
FORWARDS = {
    3: [(3, 3, 6), (3, 1, 4)],
    13: [(13, -3, 10), (13, -1, 12)],
    1: [(1, 1, 2)],
    15: [(15, -1, 14)],
    4: [(4, 1, 5)],
    12: [(12, -1, 11)],
    6: [(6, 2, 8), (6, 1, 7)],
    10: [(10, -1, 9)],
}
RELAYS = [send for sends in FORWARDS.values() for send in sends]
ARRIVALS = [
    (3, 0), (13, 0), (1, 0), (15, 0), (0, 1), (2, 0), (14, 0), (4, 0), (12, 0), (3, 1), (13, 1),
    (1, 1), (15, 1), (6, 0), (10, 0), (2, 1), (14, 1), (4, 1), (12, 1), (5, 0), (11, 0), (6, 1),
    (10, 1), (7, 0), (9, 0), (8, 0), (5, 1), (11, 1), (7, 1), (9, 1), (8, 1),
]
BOTH = (7, 8, 9)
PARTIAL_ORDER = (3, 5, 4, 7, 1, 6, 2)


def kernel(
    hid_ref, q_ref, base_ref, idx_ref, down_ref, up_ref, cache_ref, len_ref, rd_ref, rs_ref,
    out_ref,
    hid, qin, base, idx, down, up, cache, lens, rd, rs,
    part, landed, whole, kv, ids, fresh, choose, handed, q, top, acc, tot, wide,
    load_sem, tp_send, tp_recv, kv_send, kv_recv, core_send, id_send, id_recv,
    share_send, share_recv,
):
    group = lax.axis_index("group")
    ctx = lax.axis_index("ctx")
    tp = lax.axis_index("tp")
    z = ctx // 2
    x_lo = ctx % 2

    def at(step, other, core):
        side = 1 - x_lo if other else x_lo
        return {"group": core, "ctx": lax.rem(z + step + NZ, NZ) * 2 + side}

    barrier = pltpu.get_barrier_semaphore()

    def greet(peers):
        for peer in peers:
            pl.semaphore_signal(barrier, inc=1, device_id=peer, device_id_type=MESH)

    tp_peers = [{"tp": lax.rem(tp + d, NTP)} for d in range(1, NTP)]
    greet(tp_peers)

    @pl.when(group == 0)
    def _():
        greet([at(0, False, 1)])

    @pl.when(group == 1)
    def _():
        greet([at(step, False, 0) for step in (3, -3, 1, -1, 0)] + [at(0, True, 0)])
        greet([at(step, False, 1) for step in (3, -3, 2, -2, 1, -1)] + [at(0, True, 1)])
        greet([at(step, True, 1) for step in (-2, -1, 1)])

    loads = [
        pltpu.make_async_copy(src, dst, load_sem.at[i])
        for i, (src, dst) in enumerate(
            [(hid_ref, hid), (down_ref, down), (idx_ref, idx), (up_ref, up), (base_ref, base),
             (rd_ref, rd), (rs_ref, rs), (q_ref, qin), (len_ref, lens), (cache_ref, cache)]
        )
    ]
    for load in loads[:9]:
        load.start()

    @pl.when(group == 1)
    def _():
        loads[9].start()

    for load in loads[:3]:
        load.wait()

    eye = lax.broadcasted_iota(jnp.int32, (ROWS, ROWS), 0) == lax.broadcasted_iota(
        jnp.int32, (ROWS, ROWS), 1
    )
    adapter = jnp.sum(
        jnp.where(eye, jnp.broadcast_to(idx[...].astype(jnp.float32), (ROWS, ROWS)), 0.0),
        axis=1,
        keepdims=True,
    )
    shrunk = jnp.dot(hid[...], down[...], preferred_element_type=jnp.float32)
    picked = jnp.zeros((ROWS, RANK2), jnp.float32)
    for a in range(ADAPTERS):
        picked = jnp.where(adapter == float(a), shrunk[:, a * RANK2 : (a + 1) * RANK2], picked)
    part[...] = picked

    @pl.when(group == 0)
    def _():
        pl.semaphore_wait(barrier, 13)

    @pl.when(group == 1)
    def _():
        pl.semaphore_wait(barrier, 18)

    tp_copies = [
        pltpu.make_async_remote_copy(
            src_ref=part, dst_ref=landed.at[d],
            send_sem=tp_send.at[d], recv_sem=tp_recv.at[d],
            device_id=tp_peers[d - 1], device_id_type=MESH,
        )
        for d in range(1, NTP)
    ]

    def piece(index):
        return pl.ds(pl.multiple_of(index * 16, 16), 16)

    piece_copies = [
        pltpu.make_async_remote_copy(
            src_ref=part.at[piece(lax.rem(tp + d, NTP))], dst_ref=landed.at[d, :16],
            send_sem=tp_send.at[d], recv_sem=tp_recv.at[d],
            device_id=tp_peers[d - 1], device_id_type=MESH,
        )
        for d in range(1, NTP)
    ]
    share_copies = [
        pltpu.make_async_remote_copy(
            src_ref=whole.at[piece(tp)], dst_ref=whole.at[piece(tp)],
            send_sem=share_send.at[d], recv_sem=share_recv.at[d],
            device_id=tp_peers[d - 1], device_id_type=MESH,
        )
        for d in range(1, NTP)
    ]

    def id_copy(source, step, dest, side):
        i = 2 * dest + side
        return pltpu.make_async_remote_copy(
            src_ref=ids.at[source, 0], dst_ref=ids.at[dest, side],
            send_sem=id_send.at[i], recv_sem=id_recv.at[i],
            device_id=at(step, side == 1, 1), device_id_type=MESH,
        )

    @pl.when(group == 0)
    def _():
        for d in PARTIAL_ORDER:
            tp_copies[d - 1].start()

    for load in loads[3:9]:
        load.wait()

    @pl.when(group == 1)
    def _():
        ids[0, 0] = jnp.concatenate(
            [rd[...], rs[...], jnp.zeros((IDROWS - 2, ROWS), jnp.int32)], axis=0
        )
        for d in PARTIAL_ORDER:
            piece_copies[d - 1].start()
        for send in OWN_SENDS:
            id_copy(*send, 0).start()
        id_copy(0, 0, 0, 1).start()

    for g in range(GROUPS):
        for j in range(HEADS):
            q[g * 128 + j * 16 : g * 128 + (j + 1) * 16, :] = qin[
                g * 16 : (g + 1) * 16, j * HEAD : (j + 1) * HEAD
            ]
    is_key = (lax.broadcasted_iota(jnp.int32, (ADAPTERS * RANK2, HEAD), 0) // 64) % 2 == 0
    up_f = up[...].astype(jnp.float32)
    wide[:, :HEAD] = jnp.where(is_key, up_f, 0.0).astype(jnp.bfloat16)
    wide[:, HEAD:] = jnp.where(is_key, 0.0, up_f).astype(jnp.bfloat16)

    def scores_of(queries, keys):
        return lax.dot_general(
            queries, keys, (((1,), (1,)), ((), ())), preferred_element_type=jnp.float32
        )

    def weighted(weights, values):
        ones = jnp.ones(values.shape, jnp.bfloat16)
        return jnp.dot(
            weights.astype(jnp.bfloat16),
            jnp.concatenate([values, ones], axis=1),
            preferred_element_type=jnp.float32,
        )

    def first_keys(rows, scores, values):
        peak = jnp.max(scores, axis=1, keepdims=True)
        both = weighted(jnp.exp2((scores - peak) * SCALE), values)
        top[rows, :] = jnp.broadcast_to(peak, (peak.shape[0], HEAD))
        acc[rows, :] = both[:, :HEAD]
        tot[rows, :] = both[:, HEAD:]

    def more_keys(rows, scores, values):
        before = top[rows, :]
        after = jnp.maximum(before, jnp.max(scores, axis=1, keepdims=True))
        rescale = jnp.exp2((before - after) * SCALE)
        both = weighted(jnp.exp2((scores - after[:, :1]) * SCALE), values)
        top[rows, :] = after
        acc[rows, :] = acc[rows, :] * rescale + both[:, :HEAD]
        tot[rows, :] = tot[rows, :] * rescale + both[:, HEAD:]

    row16 = lax.broadcasted_iota(jnp.int32, (128, 1), 0) % 16

    @pl.when(group == 1)
    def _():
        loads[9].wait()
        column = lax.broadcasted_iota(jnp.int32, (1, CACHE), 1)
        for g in range(GROUPS):
            rows = slice(g * 128, (g + 1) * 128)
            block = cache[4 * g : 4 * g + 4].reshape(4 * CACHE, 2 * HEAD)
            scores = scores_of(q[rows, :], block[:, :HEAD])
            own = row16 // 4
            pieces = []
            for n in range(4):
                ok = jnp.logical_and(own == n, column < lens[4 * g + n])
                pieces.append(jnp.where(ok, scores[:, n * CACHE : (n + 1) * CACHE], NEG))
            first_keys(rows, jnp.concatenate(pieces, axis=1), block[:, HEAD:])

        summed = part[piece(tp), :]
        for d in range(1, NTP):
            piece_copies[d - 1].wait_recv()
            summed = summed + landed[d, :16]
        whole[piece(tp), :] = summed.astype(jnp.bfloat16)
        for d in PARTIAL_ORDER:
            share_copies[d - 1].start()
        for slot, side in ARRIVALS:
            if side == 0:
                id_copy(0, 1, slot, 0).wait_recv()
                for send in FORWARDS.get(slot, []):
                    id_copy(*send, 0).start()
                id_copy(slot, 0, slot, 1).start()
            else:
                id_copy(slot, 0, slot, 1).wait_recv()
        page = lax.broadcasted_iota(jnp.int32, (PAGES, KEYS), 0)
        key = lax.broadcasted_iota(jnp.int32, (PAGES, KEYS), 1)
        same = jnp.logical_and(page // 8 == key // ROWS, page % 8 == key % 8)
        for c in range(CHUNKS):
            slots = ORDER[c * CHUNK : (c + 1) * CHUNK]
            device = jnp.concatenate([ids[s, d, :1] for s in slots for d in (0, 1)], axis=1)
            mine = jnp.logical_and(same, device == ctx)
            choose[c] = jnp.where(mine, 1.0, 0.0).astype(jnp.bfloat16)

    def own_rows(total):
        spread = jnp.concatenate(
            [
                jnp.where(adapter == float(a), total, 0.0).astype(jnp.bfloat16)
                for a in range(ADAPTERS)
            ],
            axis=1,
        )
        delta = jnp.dot(spread, wide[...], preferred_element_type=jnp.float32)
        return (base[...].astype(jnp.float32) + delta).astype(jnp.bfloat16)

    def kv_copy(source, step, dest, side):
        i = 2 * PLACE[dest] + side
        return pltpu.make_async_remote_copy(
            src_ref=kv.at[PLACE[source], 0], dst_ref=kv.at[PLACE[dest], side],
            send_sem=kv_send.at[i], recv_sem=kv_recv.at[i],
            device_id=at(step, side == 1, 1), device_id_type=MESH,
        )

    def core_copy(slot, side):
        i = 2 * PLACE[slot] + side
        return pltpu.make_async_remote_copy(
            src_ref=kv.at[PLACE[slot], side], dst_ref=kv.at[PLACE[slot], side],
            send_sem=core_send.at[i], recv_sem=kv_recv.at[i],
            device_id={"group": 1 - group}, device_id_type=MESH,
        )

    def chunk_of(c):
        block = kv[c * CHUNK : (c + 1) * CHUNK].reshape(KEYS, 2 * HEAD)
        return block[:, :HEAD], block[:, HEAD:]

    @pl.when(group == 0)
    def _():
        total = picked
        for d in range(1, NTP):
            tp_copies[d - 1].wait_recv()
            total = total + landed[d]
        kv[0, 0] = own_rows(total)
        for send in OWN_SENDS:
            kv_copy(*send, 0).start()
        kv_copy(0, 0, 0, 1).start()
        core_copy(0, 0).start()
        for c in range(CHUNKS):
            slots = ORDER[c * CHUNK : (c + 1) * CHUNK]
            for slot in slots:
                for side in (0, 1):
                    if (slot, side) != (0, 0):
                        core_copy(slot, side).wait_recv()
            limit = [jnp.where(z >= slot, 0.0, NEG) for slot in slots for _ in (0, 1)]
            if c == 0:
                limit[1] = jnp.where(x_lo == 1, 0.0, NEG)

            def chunk(c=c, slots=slots, limit=limit):
                keys, values = chunk_of(c)
                bias = jnp.concatenate(
                    [jnp.full((1, ROWS), value, jnp.float32) for value in limit], axis=1
                )
                for g in range(GROUPS):
                    rows = slice(g * 128, (g + 1) * 128)
                    scores = scores_of(q[rows, :], keys) + bias
                    if c == 0:
                        column = lax.broadcasted_iota(jnp.int32, (1, ROWS), 1)
                        diagonal = jnp.where(column <= g * 16 + row16, scores[:, :ROWS], NEG)
                        scores = jnp.concatenate([diagonal, scores[:, ROWS:]], axis=1)
                        first_keys(rows, scores, values)
                    else:
                        more_keys(rows, scores, values)

            if c == 0:
                chunk()
            else:
                pl.when(z >= min(slots))(chunk)

    @pl.when(group == 1)
    def _():
        seen = set()
        core_copy(0, 0).wait_recv()
        seen.add((0, 0))
        ready = 0
        for slot, side in ARRIVALS:
            if side == 0:
                kv_copy(0, 1, slot, 0).wait_recv()
                for send in FORWARDS.get(slot, []):
                    kv_copy(*send, 0).start()
                    if send[2] in BOTH:
                        kv_copy(*send, 1).start()
                if slot not in BOTH:
                    kv_copy(slot, 0, slot, 1).start()
            else:
                kv_copy(slot, 0, slot, 1).wait_recv()
            core_copy(slot, side).start()
            seen.add((slot, side))
            if (slot, side) == (12, 1):
                for copy in share_copies:
                    copy.wait_recv()
                fresh[...] = own_rows(whole[...].astype(jnp.float32))
            slots = ORDER[ready * CHUNK : (ready + 1) * CHUNK]
            if all((s, d) in seen for s in slots for d in (0, 1)):
                block = kv[ready * CHUNK : (ready + 1) * CHUNK].reshape(KEYS, 2 * HEAD)
                handed[ready * PAGES : (ready + 1) * PAGES, :] = jnp.dot(
                    choose[ready], block, preferred_element_type=jnp.float32
                ).astype(jnp.bfloat16)
                ready += 1
        assert ready == CHUNKS
        codes = []
        for c in range(CHUNKS):
            slots = ORDER[c * CHUNK : (c + 1) * CHUNK]
            sequence = jnp.concatenate([ids[s, d, 1:2] for s in slots for d in (0, 1)], axis=1)
            sequence = jnp.broadcast_to(sequence.astype(jnp.float32) + 1.0, (16, KEYS))
            codes.append(scores_of(sequence.astype(jnp.bfloat16), choose[c])[:1])
        code = jnp.concatenate(codes, axis=1) - 1.0
        both = jnp.concatenate([handed[...], fresh[...]], axis=0)
        column = lax.broadcasted_iota(jnp.int32, (1, ROWS), 1)
        for g in range(GROUPS):
            rows = slice(g * 128, (g + 1) * 128)
            token = g * 16 + row16
            scores = scores_of(q[rows, :], both[:, :HEAD])
            step_ok = jnp.logical_and(column // 4 == token // 4, column <= token)
            handed_ok = code == (token // 4).astype(jnp.float32)
            scores = jnp.concatenate(
                [
                    jnp.where(handed_ok, scores[:, : CHUNKS * PAGES], NEG),
                    jnp.where(step_ok, scores[:, CHUNKS * PAGES :], NEG),
                ],
                axis=1,
            )
            more_keys(rows, scores, both[:, HEAD:])

    for g in range(GROUPS):
        rows = slice(g * 128, (g + 1) * 128)
        result = (acc[rows, :] / tot[rows, :]).astype(jnp.bfloat16)
        for j in range(HEADS):
            out_ref[g * 16 : (g + 1) * 16, j * HEAD : (j + 1) * HEAD] = result[
                j * 16 : (j + 1) * 16
            ]

    @pl.when(group == 0)
    def _():
        for copy in tp_copies:
            copy.wait_send()
        for send in OWN_SENDS:
            kv_copy(*send, 0).wait_send()
        kv_copy(0, 0, 0, 1).wait_send()
        core_copy(0, 0).wait_send()

    @pl.when(group == 1)
    def _():
        for copy in piece_copies + share_copies:
            copy.wait_send()
        for send in OWN_SENDS:
            id_copy(*send, 0).wait_send()
        id_copy(0, 0, 0, 1).wait_send()
        for send in RELAYS:
            id_copy(*send, 0).wait_send()
            kv_copy(*send, 0).wait_send()
            if send[2] in BOTH:
                kv_copy(*send, 1).wait_send()
        for slot, side in ARRIVALS:
            core_copy(slot, side).wait_send()
            if side == 0:
                id_copy(slot, 0, slot, 1).wait_send()
                if slot not in BOTH:
                    kv_copy(slot, 0, slot, 1).wait_send()


def body(hidden, queries, base, adapter, down, up, cache, lengths, device, sequence):
    vmem = pltpu.VMEM
    dma = pltpu.SemaphoreType.DMA
    bf16, f32, i32 = jnp.bfloat16, jnp.float32, jnp.int32
    out = pl.pallas_call(
        kernel,
        out_shape=jax.ShapeDtypeStruct((ROWS, HEADS * HEAD), bf16),
        in_specs=[pl.BlockSpec(memory_space=pl.ANY)] * 10,
        out_specs=pl.BlockSpec(memory_space=vmem),
        scratch_shapes=[
            vmem((ROWS, 1024), bf16),
            vmem((ROWS, HEADS * HEAD), bf16),
            vmem((ROWS, 2 * HEAD), bf16),
            vmem((1, ROWS), i32),
            vmem((1024, ADAPTERS * RANK2), bf16),
            vmem((ADAPTERS * RANK2, HEAD), bf16),
            vmem((SEQ_DEV, CACHE, 2 * HEAD), bf16),
            pltpu.SMEM((SEQ_DEV,), i32),
            vmem((1, ROWS), i32),
            vmem((1, ROWS), i32),
            vmem((ROWS, RANK2), f32),
            vmem((NTP, ROWS, RANK2), f32),
            vmem((ROWS, RANK2), bf16),
            vmem((NZ, 2, ROWS, 2 * HEAD), bf16),
            vmem((NZ, 2, IDROWS, ROWS), i32),
            vmem((ROWS, 2 * HEAD), bf16),
            vmem((CHUNKS, PAGES, KEYS), bf16),
            vmem((CHUNKS * PAGES, 2 * HEAD), bf16),
            vmem((QROWS, HEAD), bf16),
            vmem((QROWS, HEAD), f32),
            vmem((QROWS, HEAD), f32),
            vmem((QROWS, HEAD), f32),
            vmem((ADAPTERS * RANK2, 2 * HEAD), bf16),
            dma((10,)), dma((NTP,)), dma((NTP,)), dma((2 * NZ,)), dma((2 * NZ,)),
            dma((2 * NZ,)), dma((2 * NZ,)), dma((2 * NZ,)), dma((NTP,)), dma((NTP,)),
        ],
        compiler_params=pltpu.CompilerParams(
            collective_id=0, has_side_effects=True, vmem_limit_bytes=60 << 20
        ),
        name="attention",
    )(
        hidden,
        queries.reshape(ROWS, HEADS * HEAD),
        base.reshape(ROWS, 2 * HEAD),
        adapter.reshape(1, ROWS),
        down,
        up.reshape(ADAPTERS * RANK2, HEAD),
        cache.reshape(SEQ_DEV, CACHE, 2 * HEAD),
        lengths,
        device.reshape(1, ROWS),
        sequence.reshape(1, ROWS),
    )
    return out.reshape(ROWS, 1, HEADS * HEAD)


def solution(mesh):
    return jax.shard_map(
        body,
        mesh=mesh,
        in_specs=(
            P(("group", "ctx"), "tp"),
            P(("group", "ctx"), "tp", None),
            P(("group", "ctx"), "tp", None),
            P(("group", "ctx")),
            P("tp", None),
            P(None, None, None, "tp", None),
            P("ctx", None, "tp", None),
            P("ctx"),
            P("ctx", None),
            P("ctx"),
        ),
        out_specs=P(("group", "ctx"), "tp", None),
        check_vma=False,
    )
```

```python
import math

import jax
import jax.numpy as jnp
from jax import lax
from jax.experimental import pallas as pl
from jax.experimental.pallas import tpu as pltpu
from jax.sharding import PartitionSpec as P

MESH = pl.DeviceIdType.MESH
ROWS = 128
HEADS = 8
HEAD = 128
RANK2 = 128
ADAPTERS = 4
SEQ_DEV = 32
CACHE = 128
IDROWS = 8
NZ = 16
NTP = 8
QROWS = ROWS * HEADS
GROUPS = 8
NEG = -1e30
SCALE = math.log2(math.e) / math.sqrt(HEAD)

ORDER = [0, 1, 15, 3, 13, 2, 14, 4, 12, 6, 10, 5, 11, 7, 9, 8]
PLACE = {slot: i for i, slot in enumerate(ORDER)}
CHUNK = 4
CHUNKS = NZ // CHUNK
KEYS = CHUNK * 2 * ROWS
PAGES = CHUNK * 2 * 8
OWN_SENDS = [(0, 3, 3), (0, -3, 13), (0, 1, 1), (0, -1, 15)]
FORWARDS = {
    3: [(3, 3, 6), (3, 1, 4)],
    13: [(13, -3, 10), (13, -1, 12)],
    1: [(1, 1, 2)],
    15: [(15, -1, 14)],
    4: [(4, 1, 5)],
    12: [(12, -1, 11)],
    6: [(6, 2, 8), (6, 1, 7)],
    10: [(10, -1, 9)],
}
RELAYS = [send for sends in FORWARDS.values() for send in sends]
ARRIVALS = [
    (3, 0), (13, 0), (1, 0), (15, 0), (0, 1), (2, 0), (14, 0), (4, 0), (12, 0), (3, 1), (13, 1),
    (1, 1), (15, 1), (6, 0), (10, 0), (2, 1), (14, 1), (4, 1), (12, 1), (5, 0), (11, 0), (6, 1),
    (10, 1), (7, 0), (9, 0), (8, 0), (5, 1), (11, 1), (7, 1), (9, 1), (8, 1),
]
BOTH = (7, 8, 9)
LAST = 256
PARTIAL_ORDER = (3, 5, 4, 7, 1, 6, 2)


def kernel(
    hid_ref, q_ref, base_ref, idx_ref, down_ref, up_ref, cache_ref, len_ref, rd_ref, rs_ref,
    out_ref,
    hid, qin, base, idx, down, up, cache, lens, rd, rs,
    part, landed, whole, kv, ids, fresh, choose, code_row, handed, q, top, acc, tot, wide,
    load_sem, tp_send, tp_recv, kv_send, kv_recv, core_send, id_send, id_recv,
    share_send, share_recv,
):
    group = lax.axis_index("group")
    ctx = lax.axis_index("ctx")
    tp = lax.axis_index("tp")
    z = ctx // 2
    x_lo = ctx % 2

    def at(step, other, core):
        side = 1 - x_lo if other else x_lo
        return {"group": core, "ctx": lax.rem(z + step + NZ, NZ) * 2 + side}

    barrier = pltpu.get_barrier_semaphore()

    def greet(peers):
        for peer in peers:
            pl.semaphore_signal(barrier, inc=1, device_id=peer, device_id_type=MESH)

    tp_peers = [{"tp": lax.rem(tp + d, NTP)} for d in range(1, NTP)]
    greet(tp_peers)

    @pl.when(group == 0)
    def _():
        greet([at(0, False, 1)])

    @pl.when(group == 1)
    def _():
        greet([at(step, False, 0) for step in (3, -3, 1, -1, 0)] + [at(0, True, 0)])
        greet([at(step, False, 1) for step in (3, -3, 2, -2, 1, -1)] + [at(0, True, 1)])
        greet([at(step, True, 1) for step in (-2, -1, 1)])

    loads = [
        pltpu.make_async_copy(src, dst, load_sem.at[i])
        for i, (src, dst) in enumerate(
            [(hid_ref, hid), (down_ref, down), (idx_ref, idx), (up_ref, up), (base_ref, base),
             (rd_ref, rd), (rs_ref, rs), (q_ref, qin), (len_ref, lens), (cache_ref, cache)]
        )
    ]
    for load in loads[:9]:
        load.start()

    @pl.when(group == 1)
    def _():
        loads[9].start()

    for load in loads[:3]:
        load.wait()

    eye = lax.broadcasted_iota(jnp.int32, (ROWS, ROWS), 0) == lax.broadcasted_iota(
        jnp.int32, (ROWS, ROWS), 1
    )
    adapter = jnp.sum(
        jnp.where(eye, jnp.broadcast_to(idx[...].astype(jnp.float32), (ROWS, ROWS)), 0.0),
        axis=1,
        keepdims=True,
    )
    shrunk = jnp.dot(hid[...], down[...], preferred_element_type=jnp.float32)
    picked = jnp.zeros((ROWS, RANK2), jnp.float32)
    for a in range(ADAPTERS):
        picked = jnp.where(adapter == float(a), shrunk[:, a * RANK2 : (a + 1) * RANK2], picked)
    part[...] = picked

    @pl.when(group == 0)
    def _():
        pl.semaphore_wait(barrier, 13)

    @pl.when(group == 1)
    def _():
        pl.semaphore_wait(barrier, 18)

    tp_copies = [
        pltpu.make_async_remote_copy(
            src_ref=part, dst_ref=landed.at[d],
            send_sem=tp_send.at[d], recv_sem=tp_recv.at[d],
            device_id=tp_peers[d - 1], device_id_type=MESH,
        )
        for d in range(1, NTP)
    ]

    def piece(index):
        return pl.ds(pl.multiple_of(index * 16, 16), 16)

    piece_copies = [
        pltpu.make_async_remote_copy(
            src_ref=part.at[piece(lax.rem(tp + d, NTP))], dst_ref=landed.at[d, :16],
            send_sem=tp_send.at[d], recv_sem=tp_recv.at[d],
            device_id=tp_peers[d - 1], device_id_type=MESH,
        )
        for d in range(1, NTP)
    ]
    share_copies = [
        pltpu.make_async_remote_copy(
            src_ref=whole.at[piece(tp)], dst_ref=whole.at[piece(tp)],
            send_sem=share_send.at[d], recv_sem=share_recv.at[d],
            device_id=tp_peers[d - 1], device_id_type=MESH,
        )
        for d in range(1, NTP)
    ]

    def id_copy(source, step, dest, side):
        i = 2 * dest + side
        return pltpu.make_async_remote_copy(
            src_ref=ids.at[source, 0], dst_ref=ids.at[dest, side],
            send_sem=id_send.at[i], recv_sem=id_recv.at[i],
            device_id=at(step, side == 1, 1), device_id_type=MESH,
        )

    @pl.when(group == 0)
    def _():
        for d in PARTIAL_ORDER:
            tp_copies[d - 1].start()

    for load in loads[3:9]:
        load.wait()

    @pl.when(group == 1)
    def _():
        ids[0, 0] = jnp.concatenate(
            [rd[...], rs[...], jnp.zeros((IDROWS - 2, ROWS), jnp.int32)], axis=0
        )
        for d in PARTIAL_ORDER:
            piece_copies[d - 1].start()
        for send in OWN_SENDS:
            id_copy(*send, 0).start()
        id_copy(0, 0, 0, 1).start()

    for g in range(GROUPS):
        for j in range(HEADS):
            q[g * 128 + j * 16 : g * 128 + (j + 1) * 16, :] = qin[
                g * 16 : (g + 1) * 16, j * HEAD : (j + 1) * HEAD
            ]
    is_key = (lax.broadcasted_iota(jnp.int32, (ADAPTERS * RANK2, HEAD), 0) // 64) % 2 == 0
    up_f = up[...].astype(jnp.float32)
    wide[:, :HEAD] = jnp.where(is_key, up_f, 0.0).astype(jnp.bfloat16)
    wide[:, HEAD:] = jnp.where(is_key, 0.0, up_f).astype(jnp.bfloat16)

    def scores_of(queries, keys):
        return lax.dot_general(
            queries, keys, (((1,), (1,)), ((), ())), preferred_element_type=jnp.float32
        )

    def weighted(weights, values):
        ones = jnp.ones(values.shape, jnp.bfloat16)
        return jnp.dot(
            weights.astype(jnp.bfloat16),
            jnp.concatenate([values, ones], axis=1),
            preferred_element_type=jnp.float32,
        )

    def first_keys(rows, scores, values):
        peak = jnp.max(scores, axis=1, keepdims=True)
        both = weighted(jnp.exp2((scores - peak) * SCALE), values)
        top[rows, :] = jnp.broadcast_to(peak, (peak.shape[0], HEAD))
        acc[rows, :] = both[:, :HEAD]
        tot[rows, :] = both[:, HEAD:]

    def more_keys(rows, scores, values):
        before = top[rows, :]
        after = jnp.maximum(before, jnp.max(scores, axis=1, keepdims=True))
        rescale = jnp.exp2((before - after) * SCALE)
        both = weighted(jnp.exp2((scores - after[:, :1]) * SCALE), values)
        top[rows, :] = after
        acc[rows, :] = acc[rows, :] * rescale + both[:, :HEAD]
        tot[rows, :] = tot[rows, :] * rescale + both[:, HEAD:]

    def emit(group_row, result):
        for g in range(result.shape[0] // 128):
            first = (group_row + g) * 16
            for j in range(HEADS):
                start = g * 128 + j * 16
                out_ref[first : first + 16, j * HEAD : (j + 1) * HEAD] = result[start : start + 16]

    row16 = lax.broadcasted_iota(jnp.int32, (128, 1), 0) % 16

    def own_rows(total):
        spread = jnp.concatenate(
            [
                jnp.where(adapter == float(a), total, 0.0).astype(jnp.bfloat16)
                for a in range(ADAPTERS)
            ],
            axis=1,
        )
        delta = jnp.dot(spread, wide[...], preferred_element_type=jnp.float32)
        return (base[...].astype(jnp.float32) + delta).astype(jnp.bfloat16)

    @pl.when(group == 1)
    def _():
        loads[9].wait()
        column = lax.broadcasted_iota(jnp.int32, (1, CACHE), 1)
        for g in range(GROUPS):
            rows = slice(g * 128, (g + 1) * 128)
            block = cache[4 * g : 4 * g + 4].reshape(4 * CACHE, 2 * HEAD)
            scores = scores_of(q[rows, :], block[:, :HEAD])
            own = row16 // 4
            pieces = []
            for n in range(4):
                ok = jnp.logical_and(own == n, column < lens[4 * g + n])
                pieces.append(jnp.where(ok, scores[:, n * CACHE : (n + 1) * CACHE], NEG))
            first_keys(rows, jnp.concatenate(pieces, axis=1), block[:, HEAD:])

        summed = part[piece(tp), :]
        for d in range(1, NTP):
            piece_copies[d - 1].wait_recv()
            summed = summed + landed[d, :16]
        whole[piece(tp), :] = summed.astype(jnp.bfloat16)
        for d in PARTIAL_ORDER:
            share_copies[d - 1].start()
        for slot, side in ARRIVALS:
            if side == 0:
                id_copy(0, 1, slot, 0).wait_recv()
                for send in FORWARDS.get(slot, []):
                    id_copy(*send, 0).start()
                id_copy(slot, 0, slot, 1).start()
            else:
                id_copy(slot, 0, slot, 1).wait_recv()
            if (slot, side) == (5, 1):
                for copy in share_copies:
                    copy.wait_recv()
                fresh[...] = own_rows(whole[...].astype(jnp.float32))
        page = lax.broadcasted_iota(jnp.int32, (PAGES, KEYS), 0)
        key = lax.broadcasted_iota(jnp.int32, (PAGES, KEYS), 1)
        same = jnp.logical_and(page // 8 == key // ROWS, page % 8 == key % 8)
        spread8 = lax.broadcasted_iota(
            jnp.int32, (2 * CHUNK, PAGES), 0
        ) == lax.broadcasted_iota(jnp.int32, (2 * CHUNK, PAGES), 1) // 8
        codes = []
        for c in range(CHUNKS):
            slots = ORDER[c * CHUNK : (c + 1) * CHUNK]
            device = jnp.concatenate([ids[s, d, :1] for s in slots for d in (0, 1)], axis=1)
            mine = jnp.logical_and(same, device == ctx)
            choose[c] = jnp.where(mine, 1.0, 0.0).astype(jnp.bfloat16)
            device = jnp.concatenate([ids[s, d, :1] for s in slots for d in (0, 1)], axis=0)
            sequence = jnp.concatenate([ids[s, d, 1:2] for s in slots for d in (0, 1)], axis=0)
            sequence = jnp.where(device == ctx, sequence, -1).astype(jnp.float32)
            sequence = jnp.max(sequence, axis=1, keepdims=True)
            codes.append(jnp.sum(jnp.where(spread8, sequence, 0.0), axis=0, keepdims=True))
        code_row[...] = jnp.broadcast_to(jnp.concatenate(codes, axis=1), code_row.shape)

    def kv_copy(source, step, dest, side):
        i = 2 * PLACE[dest] + side
        return pltpu.make_async_remote_copy(
            src_ref=kv.at[PLACE[source], 0], dst_ref=kv.at[PLACE[dest], side],
            send_sem=kv_send.at[i], recv_sem=kv_recv.at[i],
            device_id=at(step, side == 1, 1), device_id_type=MESH,
        )

    def core_copy(slot, side):
        i = 2 * PLACE[slot] + side
        return pltpu.make_async_remote_copy(
            src_ref=kv.at[PLACE[slot], side], dst_ref=kv.at[PLACE[slot], side],
            send_sem=core_send.at[i], recv_sem=kv_recv.at[i],
            device_id={"group": 1 - group}, device_id_type=MESH,
        )

    def chunk_of(c):
        block = kv[c * CHUNK : (c + 1) * CHUNK].reshape(KEYS, 2 * HEAD)
        return block[:, :HEAD], block[:, HEAD:]

    @pl.when(group == 0)
    def _():
        total = picked
        for d in range(1, NTP):
            tp_copies[d - 1].wait_recv()
            total = total + landed[d]
        kv[0, 0] = own_rows(total)
        for send in OWN_SENDS:
            kv_copy(*send, 0).start()
        kv_copy(0, 0, 0, 1).start()
        core_copy(0, 0).start()
        for c in range(CHUNKS):
            slots = ORDER[c * CHUNK : (c + 1) * CHUNK]
            for slot in slots:
                for side in (0, 1):
                    if (slot, side) != (0, 0):
                        core_copy(slot, side).wait_recv()
            limit = [jnp.where(z >= slot, 0.0, NEG) for slot in slots for _ in (0, 1)]
            if c == 0:
                limit[1] = jnp.where(x_lo == 1, 0.0, NEG)

            def chunk(c=c, slots=slots, limit=limit):
                keys, values = chunk_of(c)
                bias = jnp.concatenate(
                    [jnp.full((1, ROWS), value, jnp.float32) for value in limit], axis=1
                )
                for g in range(GROUPS):
                    rows = slice(g * 128, (g + 1) * 128)
                    scores = scores_of(q[rows, :], keys) + bias
                    if c == 0:
                        column = lax.broadcasted_iota(jnp.int32, (1, ROWS), 1)
                        diagonal = jnp.where(column <= g * 16 + row16, scores[:, :ROWS], NEG)
                        scores = jnp.concatenate([diagonal, scores[:, ROWS:]], axis=1)
                        first_keys(rows, scores, values)
                    else:
                        more_keys(rows, scores, values)

            if c == 0:
                chunk()
            else:
                pl.when(z >= min(slots))(chunk)

    @pl.when(group == 1)
    def _():
        seen = set()
        core_copy(0, 0).wait_recv()
        seen.add((0, 0))
        ready = 0
        for slot, side in ARRIVALS:
            if side == 0:
                kv_copy(0, 1, slot, 0).wait_recv()
                for send in FORWARDS.get(slot, []):
                    kv_copy(*send, 0).start()
                    if send[2] in BOTH:
                        kv_copy(*send, 1).start()
                if slot not in BOTH:
                    kv_copy(slot, 0, slot, 1).start()
            else:
                kv_copy(slot, 0, slot, 1).wait_recv()
            core_copy(slot, side).start()
            seen.add((slot, side))
            slots = ORDER[ready * CHUNK : (ready + 1) * CHUNK]
            if all((s, d) in seen for s in slots for d in (0, 1)):
                block = kv[ready * CHUNK : (ready + 1) * CHUNK].reshape(KEYS, 2 * HEAD)
                handed[ready * PAGES : (ready + 1) * PAGES, :] = jnp.dot(
                    choose[ready], block, preferred_element_type=jnp.float32
                ).astype(jnp.bfloat16)
                ready += 1
        assert ready == CHUNKS
        code = code_row[:1, :]
        both = jnp.concatenate([handed[...], fresh[...]], axis=0)
        column = lax.broadcasted_iota(jnp.int32, (1, ROWS), 1)
        row = lax.broadcasted_iota(jnp.int32, (LAST, 1), 0)
        for i in range(QROWS // LAST):
            rows = slice(i * LAST, (i + 1) * LAST)
            token = (i * (LAST // 128) + row // 128) * 16 + row % 16
            scores = scores_of(q[rows, :], both[:, :HEAD])
            step_ok = jnp.logical_and(column // 4 == token // 4, column <= token)
            handed_ok = code == (token // 4).astype(jnp.float32)
            scores = jnp.concatenate(
                [
                    jnp.where(handed_ok, scores[:, : CHUNKS * PAGES], NEG),
                    jnp.where(step_ok, scores[:, CHUNKS * PAGES :], NEG),
                ],
                axis=1,
            )
            before = top[rows, :]
            after = jnp.maximum(before, jnp.max(scores, axis=1, keepdims=True))
            rescale = jnp.exp2((before - after) * SCALE)
            sums = weighted(jnp.exp2((scores - after[:, :1]) * SCALE), both[:, HEAD:])
            total = tot[rows, :] * rescale + sums[:, HEAD:]
            result = (acc[rows, :] * rescale + sums[:, :HEAD]) / total
            emit(i * (LAST // 128), result.astype(jnp.bfloat16))

    @pl.when(group == 0)
    def _():
        for g in range(GROUPS):
            rows = slice(g * 128, (g + 1) * 128)
            emit(g, (acc[rows, :] / tot[rows, :]).astype(jnp.bfloat16))

    @pl.when(group == 0)
    def _():
        for copy in tp_copies:
            copy.wait_send()
        for send in OWN_SENDS:
            kv_copy(*send, 0).wait_send()
        kv_copy(0, 0, 0, 1).wait_send()
        core_copy(0, 0).wait_send()

    @pl.when(group == 1)
    def _():
        for copy in piece_copies + share_copies:
            copy.wait_send()
        for send in OWN_SENDS:
            id_copy(*send, 0).wait_send()
        id_copy(0, 0, 0, 1).wait_send()
        for send in RELAYS:
            id_copy(*send, 0).wait_send()
            kv_copy(*send, 0).wait_send()
            if send[2] in BOTH:
                kv_copy(*send, 1).wait_send()
        for slot, side in ARRIVALS:
            core_copy(slot, side).wait_send()
            if side == 0:
                id_copy(slot, 0, slot, 1).wait_send()
                if slot not in BOTH:
                    kv_copy(slot, 0, slot, 1).wait_send()


def body(hidden, queries, base, adapter, down, up, cache, lengths, device, sequence):
    vmem = pltpu.VMEM
    dma = pltpu.SemaphoreType.DMA
    bf16, f32, i32 = jnp.bfloat16, jnp.float32, jnp.int32
    out = pl.pallas_call(
        kernel,
        out_shape=jax.ShapeDtypeStruct((ROWS, HEADS * HEAD), bf16),
        in_specs=[pl.BlockSpec(memory_space=pl.ANY)] * 10,
        out_specs=pl.BlockSpec(memory_space=vmem),
        scratch_shapes=[
            vmem((ROWS, 1024), bf16),
            vmem((ROWS, HEADS * HEAD), bf16),
            vmem((ROWS, 2 * HEAD), bf16),
            vmem((1, ROWS), i32),
            vmem((1024, ADAPTERS * RANK2), bf16),
            vmem((ADAPTERS * RANK2, HEAD), bf16),
            vmem((SEQ_DEV, CACHE, 2 * HEAD), bf16),
            pltpu.SMEM((SEQ_DEV,), i32),
            vmem((1, ROWS), i32),
            vmem((1, ROWS), i32),
            vmem((ROWS, RANK2), f32),
            vmem((NTP, ROWS, RANK2), f32),
            vmem((ROWS, RANK2), bf16),
            vmem((NZ, 2, ROWS, 2 * HEAD), bf16),
            vmem((NZ, 2, IDROWS, ROWS), i32),
            vmem((ROWS, 2 * HEAD), bf16),
            vmem((CHUNKS, PAGES, KEYS), bf16),
            vmem((8, CHUNKS * PAGES), f32),
            vmem((CHUNKS * PAGES, 2 * HEAD), bf16),
            vmem((QROWS, HEAD), bf16),
            vmem((QROWS, HEAD), f32),
            vmem((QROWS, HEAD), f32),
            vmem((QROWS, HEAD), f32),
            vmem((ADAPTERS * RANK2, 2 * HEAD), bf16),
            dma((10,)), dma((NTP,)), dma((NTP,)), dma((2 * NZ,)), dma((2 * NZ,)),
            dma((2 * NZ,)), dma((2 * NZ,)), dma((2 * NZ,)), dma((NTP,)), dma((NTP,)),
        ],
        compiler_params=pltpu.CompilerParams(
            collective_id=0, has_side_effects=True, vmem_limit_bytes=60 << 20
        ),
        name="attention",
    )(
        hidden,
        queries.reshape(ROWS, HEADS * HEAD),
        base.reshape(ROWS, 2 * HEAD),
        adapter.reshape(1, ROWS),
        down,
        up.reshape(ADAPTERS * RANK2, HEAD),
        cache.reshape(SEQ_DEV, CACHE, 2 * HEAD),
        lengths,
        device.reshape(1, ROWS),
        sequence.reshape(1, ROWS),
    )
    return out.reshape(ROWS, 1, HEADS * HEAD)


def solution(mesh):
    return jax.shard_map(
        body,
        mesh=mesh,
        in_specs=(
            P(("group", "ctx"), "tp"),
            P(("group", "ctx"), "tp", None),
            P(("group", "ctx"), "tp", None),
            P(("group", "ctx")),
            P("tp", None),
            P(None, None, None, "tp", None),
            P("ctx", None, "tp", None),
            P("ctx"),
            P("ctx", None),
            P("ctx"),
        ),
        out_specs=P(("group", "ctx"), "tp", None),
        check_vma=False,
    )
```

```python
import math

import jax
import jax.numpy as jnp
from jax import lax
from jax.experimental import pallas as pl
from jax.experimental.pallas import tpu as pltpu
from jax.sharding import PartitionSpec as P

MESH = pl.DeviceIdType.MESH
ROWS = 128
HEADS = 8
HEAD = 128
RANK2 = 128
ADAPTERS = 4
SEQ_DEV = 32
CACHE = 128
IDROWS = 8
NZ = 16
NTP = 8
QROWS = ROWS * HEADS
GROUPS = 8
NEG = -1e30
SCALE = math.log2(math.e) / math.sqrt(HEAD)

ORDER = [0, 1, 15, 3, 13, 2, 14, 4, 12, 6, 10, 5, 11, 7, 9, 8]
PLACE = {slot: i for i, slot in enumerate(ORDER)}
CHUNK = 4
CHUNKS = NZ // CHUNK
KEYS = CHUNK * 2 * ROWS
PAGES = CHUNK * 2 * 8
OWN_SENDS = [(0, 3, 3), (0, -3, 13), (0, 1, 1), (0, -1, 15)]
FORWARDS = {
    3: [(3, 3, 6), (3, 1, 4)],
    13: [(13, -3, 10), (13, -1, 12)],
    1: [(1, 1, 2)],
    15: [(15, -1, 14)],
    4: [(4, 1, 5)],
    12: [(12, -1, 11)],
    6: [(6, 2, 8), (6, 1, 7)],
    10: [(10, -1, 9)],
}
RELAYS = [send for sends in FORWARDS.values() for send in sends]
ARRIVALS = [
    (3, 0), (13, 0), (1, 0), (15, 0), (4, 0), (12, 0), (2, 0), (14, 0), (6, 0), (10, 0), (0, 1),
    (3, 1), (13, 1), (1, 1), (15, 1), (5, 0), (11, 0), (2, 1), (14, 1), (4, 1), (12, 1), (6, 1),
    (10, 1), (7, 0), (9, 0), (8, 0), (5, 1), (11, 1), (7, 1), (9, 1), (8, 1),
]
BOTH = (7, 8, 9)
LAST = 256
PARTIAL_ORDER = (3, 5, 4, 7, 1, 6, 2)


def kernel(
    hid_ref, q_ref, base_ref, idx_ref, down_ref, up_ref, cache_ref, len_ref, rd_ref, rs_ref,
    out_ref,
    hid, qin, base, idx, down, up, cache, lens, rd, rs,
    part, landed, whole, kv, ids, fresh, choose, code_row, handed, q, top, acc, tot, wide,
    load_sem, tp_send, tp_recv, kv_send, kv_recv, core_send, id_send, id_recv,
    share_send, share_recv,
):
    group = lax.axis_index("group")
    ctx = lax.axis_index("ctx")
    tp = lax.axis_index("tp")
    z = ctx // 2
    x_lo = ctx % 2

    def at(step, other, core):
        side = 1 - x_lo if other else x_lo
        return {"group": core, "ctx": lax.rem(z + step + NZ, NZ) * 2 + side}

    barrier = pltpu.get_barrier_semaphore()

    def greet(peers):
        for peer in peers:
            pl.semaphore_signal(barrier, inc=1, device_id=peer, device_id_type=MESH)

    tp_peers = [{"tp": lax.rem(tp + d, NTP)} for d in range(1, NTP)]
    greet(tp_peers)

    @pl.when(group == 0)
    def _():
        greet([at(0, False, 1)])

    @pl.when(group == 1)
    def _():
        greet([at(step, False, 0) for step in (3, -3, 1, -1, 0)] + [at(0, True, 0)])
        greet([at(step, False, 1) for step in (3, -3, 2, -2, 1, -1)] + [at(0, True, 1)])
        greet([at(step, True, 1) for step in (-2, -1, 1)])

    loads = [
        pltpu.make_async_copy(src, dst, load_sem.at[i])
        for i, (src, dst) in enumerate(
            [(hid_ref, hid), (down_ref, down), (idx_ref, idx), (up_ref, up), (base_ref, base),
             (rd_ref, rd), (rs_ref, rs), (q_ref, qin), (len_ref, lens), (cache_ref, cache)]
        )
    ]
    for load in loads[:9]:
        load.start()

    @pl.when(group == 1)
    def _():
        loads[9].start()

    for load in loads[:3]:
        load.wait()

    eye = lax.broadcasted_iota(jnp.int32, (ROWS, ROWS), 0) == lax.broadcasted_iota(
        jnp.int32, (ROWS, ROWS), 1
    )
    adapter = jnp.sum(
        jnp.where(eye, jnp.broadcast_to(idx[...].astype(jnp.float32), (ROWS, ROWS)), 0.0),
        axis=1,
        keepdims=True,
    )
    shrunk = jnp.dot(hid[...], down[...], preferred_element_type=jnp.float32)
    picked = jnp.zeros((ROWS, RANK2), jnp.float32)
    for a in range(ADAPTERS):
        picked = jnp.where(adapter == float(a), shrunk[:, a * RANK2 : (a + 1) * RANK2], picked)
    part[...] = picked

    @pl.when(group == 0)
    def _():
        pl.semaphore_wait(barrier, 13)

    @pl.when(group == 1)
    def _():
        pl.semaphore_wait(barrier, 18)

    tp_copies = [
        pltpu.make_async_remote_copy(
            src_ref=part, dst_ref=landed.at[d],
            send_sem=tp_send.at[d], recv_sem=tp_recv.at[d],
            device_id=tp_peers[d - 1], device_id_type=MESH,
        )
        for d in range(1, NTP)
    ]

    def piece(index):
        return pl.ds(pl.multiple_of(index * 16, 16), 16)

    piece_copies = [
        pltpu.make_async_remote_copy(
            src_ref=part.at[piece(lax.rem(tp + d, NTP))], dst_ref=landed.at[d, :16],
            send_sem=tp_send.at[d], recv_sem=tp_recv.at[d],
            device_id=tp_peers[d - 1], device_id_type=MESH,
        )
        for d in range(1, NTP)
    ]
    share_copies = [
        pltpu.make_async_remote_copy(
            src_ref=whole.at[piece(tp)], dst_ref=whole.at[piece(tp)],
            send_sem=share_send.at[d], recv_sem=share_recv.at[d],
            device_id=tp_peers[d - 1], device_id_type=MESH,
        )
        for d in range(1, NTP)
    ]

    def id_copy(source, step, dest, side):
        i = 2 * dest + side
        return pltpu.make_async_remote_copy(
            src_ref=ids.at[source, 0], dst_ref=ids.at[dest, side],
            send_sem=id_send.at[i], recv_sem=id_recv.at[i],
            device_id=at(step, side == 1, 1), device_id_type=MESH,
        )

    @pl.when(group == 0)
    def _():
        for d in PARTIAL_ORDER:
            tp_copies[d - 1].start()

    for load in loads[3:9]:
        load.wait()

    @pl.when(group == 1)
    def _():
        ids[0, 0] = jnp.concatenate(
            [rd[...], rs[...], jnp.zeros((IDROWS - 2, ROWS), jnp.int32)], axis=0
        )
        for d in PARTIAL_ORDER:
            piece_copies[d - 1].start()
        for send in OWN_SENDS:
            id_copy(*send, 0).start()
        id_copy(0, 0, 0, 1).start()

    for g in range(GROUPS):
        for j in range(HEADS):
            q[g * 128 + j * 16 : g * 128 + (j + 1) * 16, :] = qin[
                g * 16 : (g + 1) * 16, j * HEAD : (j + 1) * HEAD
            ]
    is_key = (lax.broadcasted_iota(jnp.int32, (ADAPTERS * RANK2, HEAD), 0) // 64) % 2 == 0
    up_f = up[...].astype(jnp.float32)
    wide[:, :HEAD] = jnp.where(is_key, up_f, 0.0).astype(jnp.bfloat16)
    wide[:, HEAD:] = jnp.where(is_key, 0.0, up_f).astype(jnp.bfloat16)

    def scores_of(queries, keys):
        return lax.dot_general(
            queries, keys, (((1,), (1,)), ((), ())), preferred_element_type=jnp.float32
        )

    def weighted(weights, values):
        ones = jnp.ones(values.shape, jnp.bfloat16)
        return jnp.dot(
            weights.astype(jnp.bfloat16),
            jnp.concatenate([values, ones], axis=1),
            preferred_element_type=jnp.float32,
        )

    def first_keys(rows, scores, values):
        peak = jnp.max(scores, axis=1, keepdims=True)
        both = weighted(jnp.exp2((scores - peak) * SCALE), values)
        top[rows, :] = jnp.broadcast_to(peak, (peak.shape[0], HEAD))
        acc[rows, :] = both[:, :HEAD]
        tot[rows, :] = both[:, HEAD:]

    def more_keys(rows, scores, values):
        before = top[rows, :]
        after = jnp.maximum(before, jnp.max(scores, axis=1, keepdims=True))
        rescale = jnp.exp2((before - after) * SCALE)
        both = weighted(jnp.exp2((scores - after[:, :1]) * SCALE), values)
        top[rows, :] = after
        acc[rows, :] = acc[rows, :] * rescale + both[:, :HEAD]
        tot[rows, :] = tot[rows, :] * rescale + both[:, HEAD:]

    def emit(group_row, result):
        for g in range(result.shape[0] // 128):
            first = (group_row + g) * 16
            for j in range(HEADS):
                start = g * 128 + j * 16
                out_ref[first : first + 16, j * HEAD : (j + 1) * HEAD] = result[start : start + 16]

    row16 = lax.broadcasted_iota(jnp.int32, (128, 1), 0) % 16

    def own_rows(total):
        spread = jnp.concatenate(
            [
                jnp.where(adapter == float(a), total, 0.0).astype(jnp.bfloat16)
                for a in range(ADAPTERS)
            ],
            axis=1,
        )
        delta = jnp.dot(spread, wide[...], preferred_element_type=jnp.float32)
        return (base[...].astype(jnp.float32) + delta).astype(jnp.bfloat16)

    @pl.when(group == 1)
    def _():
        loads[9].wait()
        column = lax.broadcasted_iota(jnp.int32, (1, CACHE), 1)
        for g in range(GROUPS):
            rows = slice(g * 128, (g + 1) * 128)
            block = cache[4 * g : 4 * g + 4].reshape(4 * CACHE, 2 * HEAD)
            scores = scores_of(q[rows, :], block[:, :HEAD])
            own = row16 // 4
            pieces = []
            for n in range(4):
                ok = jnp.logical_and(own == n, column < lens[4 * g + n])
                pieces.append(jnp.where(ok, scores[:, n * CACHE : (n + 1) * CACHE], NEG))
            first_keys(rows, jnp.concatenate(pieces, axis=1), block[:, HEAD:])

        summed = part[piece(tp), :]
        for d in range(1, NTP):
            piece_copies[d - 1].wait_recv()
            summed = summed + landed[d, :16]
        whole[piece(tp), :] = summed.astype(jnp.bfloat16)
        for d in PARTIAL_ORDER:
            share_copies[d - 1].start()
        for slot, side in ARRIVALS:
            if side == 0:
                id_copy(0, 1, slot, 0).wait_recv()
                for send in FORWARDS.get(slot, []):
                    id_copy(*send, 0).start()
                id_copy(slot, 0, slot, 1).start()
            else:
                id_copy(slot, 0, slot, 1).wait_recv()
            if (slot, side) == (5, 1):
                for copy in share_copies:
                    copy.wait_recv()
                fresh[...] = own_rows(whole[...].astype(jnp.float32))
        page = lax.broadcasted_iota(jnp.int32, (PAGES, KEYS), 0)
        key = lax.broadcasted_iota(jnp.int32, (PAGES, KEYS), 1)
        same = jnp.logical_and(page // 8 == key // ROWS, page % 8 == key % 8)
        spread8 = lax.broadcasted_iota(
            jnp.int32, (2 * CHUNK, PAGES), 0
        ) == lax.broadcasted_iota(jnp.int32, (2 * CHUNK, PAGES), 1) // 8
        codes = []
        for c in range(CHUNKS):
            slots = ORDER[c * CHUNK : (c + 1) * CHUNK]
            device = jnp.concatenate([ids[s, d, :1] for s in slots for d in (0, 1)], axis=1)
            mine = jnp.logical_and(same, device == ctx)
            choose[c] = jnp.where(mine, 1.0, 0.0).astype(jnp.bfloat16)
            device = jnp.concatenate([ids[s, d, :1] for s in slots for d in (0, 1)], axis=0)
            sequence = jnp.concatenate([ids[s, d, 1:2] for s in slots for d in (0, 1)], axis=0)
            sequence = jnp.where(device == ctx, sequence, -1).astype(jnp.float32)
            sequence = jnp.max(sequence, axis=1, keepdims=True)
            codes.append(jnp.sum(jnp.where(spread8, sequence, 0.0), axis=0, keepdims=True))
        code_row[...] = jnp.broadcast_to(jnp.concatenate(codes, axis=1), code_row.shape)

    def kv_copy(source, step, dest, side):
        i = 2 * PLACE[dest] + side
        return pltpu.make_async_remote_copy(
            src_ref=kv.at[PLACE[source], 0], dst_ref=kv.at[PLACE[dest], side],
            send_sem=kv_send.at[i], recv_sem=kv_recv.at[i],
            device_id=at(step, side == 1, 1), device_id_type=MESH,
        )

    def core_copy(slot, side):
        i = 2 * PLACE[slot] + side
        return pltpu.make_async_remote_copy(
            src_ref=kv.at[PLACE[slot], side], dst_ref=kv.at[PLACE[slot], side],
            send_sem=core_send.at[i], recv_sem=kv_recv.at[i],
            device_id={"group": 1 - group}, device_id_type=MESH,
        )

    def chunk_of(c):
        block = kv[c * CHUNK : (c + 1) * CHUNK].reshape(KEYS, 2 * HEAD)
        return block[:, :HEAD], block[:, HEAD:]

    @pl.when(group == 0)
    def _():
        total = picked
        for d in range(1, NTP):
            tp_copies[d - 1].wait_recv()
            total = total + landed[d]
        kv[0, 0] = own_rows(total)
        for send in OWN_SENDS:
            kv_copy(*send, 0).start()
        kv_copy(0, 0, 0, 1).start()
        core_copy(0, 0).start()
        for c in range(CHUNKS):
            slots = ORDER[c * CHUNK : (c + 1) * CHUNK]
            for slot in slots:
                for side in (0, 1):
                    if (slot, side) != (0, 0):
                        core_copy(slot, side).wait_recv()
            limit = [jnp.where(z >= slot, 0.0, NEG) for slot in slots for _ in (0, 1)]
            if c == 0:
                limit[1] = jnp.where(x_lo == 1, 0.0, NEG)

            def chunk(c=c, slots=slots, limit=limit):
                keys, values = chunk_of(c)
                bias = jnp.concatenate(
                    [jnp.full((1, ROWS), value, jnp.float32) for value in limit], axis=1
                )
                for g in range(GROUPS):
                    rows = slice(g * 128, (g + 1) * 128)
                    scores = scores_of(q[rows, :], keys) + bias
                    if c == 0:
                        column = lax.broadcasted_iota(jnp.int32, (1, ROWS), 1)
                        diagonal = jnp.where(column <= g * 16 + row16, scores[:, :ROWS], NEG)
                        scores = jnp.concatenate([diagonal, scores[:, ROWS:]], axis=1)
                        first_keys(rows, scores, values)
                    else:
                        more_keys(rows, scores, values)

            if c == 0:
                chunk()
            else:
                pl.when(z >= min(slots))(chunk)

    @pl.when(group == 1)
    def _():
        seen = set()
        core_copy(0, 0).wait_recv()
        seen.add((0, 0))
        ready = 0
        for slot, side in ARRIVALS:
            if side == 0:
                kv_copy(0, 1, slot, 0).wait_recv()
                for send in FORWARDS.get(slot, []):
                    kv_copy(*send, 0).start()
                    if send[2] in BOTH:
                        kv_copy(*send, 1).start()
                if slot not in BOTH:
                    kv_copy(slot, 0, slot, 1).start()
            else:
                kv_copy(slot, 0, slot, 1).wait_recv()
            core_copy(slot, side).start()
            seen.add((slot, side))
            slots = ORDER[ready * CHUNK : (ready + 1) * CHUNK]
            if all((s, d) in seen for s in slots for d in (0, 1)):
                block = kv[ready * CHUNK : (ready + 1) * CHUNK].reshape(KEYS, 2 * HEAD)
                handed[ready * PAGES : (ready + 1) * PAGES, :] = jnp.dot(
                    choose[ready], block, preferred_element_type=jnp.float32
                ).astype(jnp.bfloat16)
                ready += 1
        assert ready == CHUNKS
        code = code_row[:1, :]
        both = jnp.concatenate([handed[...], fresh[...]], axis=0)
        column = lax.broadcasted_iota(jnp.int32, (1, ROWS), 1)
        row = lax.broadcasted_iota(jnp.int32, (LAST, 1), 0)
        for i in range(QROWS // LAST):
            rows = slice(i * LAST, (i + 1) * LAST)
            token = (i * (LAST // 128) + row // 128) * 16 + row % 16
            scores = scores_of(q[rows, :], both[:, :HEAD])
            step_ok = jnp.logical_and(column // 4 == token // 4, column <= token)
            handed_ok = code == (token // 4).astype(jnp.float32)
            scores = jnp.concatenate(
                [
                    jnp.where(handed_ok, scores[:, : CHUNKS * PAGES], NEG),
                    jnp.where(step_ok, scores[:, CHUNKS * PAGES :], NEG),
                ],
                axis=1,
            )
            before = top[rows, :]
            after = jnp.maximum(before, jnp.max(scores, axis=1, keepdims=True))
            rescale = jnp.exp2((before - after) * SCALE)
            sums = weighted(jnp.exp2((scores - after[:, :1]) * SCALE), both[:, HEAD:])
            total = tot[rows, :] * rescale + sums[:, HEAD:]
            result = (acc[rows, :] * rescale + sums[:, :HEAD]) / total
            emit(i * (LAST // 128), result.astype(jnp.bfloat16))

    @pl.when(group == 0)
    def _():
        for g in range(GROUPS):
            rows = slice(g * 128, (g + 1) * 128)
            emit(g, (acc[rows, :] / tot[rows, :]).astype(jnp.bfloat16))

    @pl.when(group == 0)
    def _():
        for copy in tp_copies:
            copy.wait_send()
        for send in OWN_SENDS:
            kv_copy(*send, 0).wait_send()
        kv_copy(0, 0, 0, 1).wait_send()
        core_copy(0, 0).wait_send()

    @pl.when(group == 1)
    def _():
        for copy in piece_copies + share_copies:
            copy.wait_send()
        for send in OWN_SENDS:
            id_copy(*send, 0).wait_send()
        id_copy(0, 0, 0, 1).wait_send()
        for send in RELAYS:
            id_copy(*send, 0).wait_send()
            kv_copy(*send, 0).wait_send()
            if send[2] in BOTH:
                kv_copy(*send, 1).wait_send()
        for slot, side in ARRIVALS:
            core_copy(slot, side).wait_send()
            if side == 0:
                id_copy(slot, 0, slot, 1).wait_send()
                if slot not in BOTH:
                    kv_copy(slot, 0, slot, 1).wait_send()


def body(hidden, queries, base, adapter, down, up, cache, lengths, device, sequence):
    vmem = pltpu.VMEM
    dma = pltpu.SemaphoreType.DMA
    bf16, f32, i32 = jnp.bfloat16, jnp.float32, jnp.int32
    out = pl.pallas_call(
        kernel,
        out_shape=jax.ShapeDtypeStruct((ROWS, HEADS * HEAD), bf16),
        in_specs=[pl.BlockSpec(memory_space=pl.ANY)] * 10,
        out_specs=pl.BlockSpec(memory_space=vmem),
        scratch_shapes=[
            vmem((ROWS, 1024), bf16),
            vmem((ROWS, HEADS * HEAD), bf16),
            vmem((ROWS, 2 * HEAD), bf16),
            vmem((1, ROWS), i32),
            vmem((1024, ADAPTERS * RANK2), bf16),
            vmem((ADAPTERS * RANK2, HEAD), bf16),
            vmem((SEQ_DEV, CACHE, 2 * HEAD), bf16),
            pltpu.SMEM((SEQ_DEV,), i32),
            vmem((1, ROWS), i32),
            vmem((1, ROWS), i32),
            vmem((ROWS, RANK2), f32),
            vmem((NTP, ROWS, RANK2), f32),
            vmem((ROWS, RANK2), bf16),
            vmem((NZ, 2, ROWS, 2 * HEAD), bf16),
            vmem((NZ, 2, IDROWS, ROWS), i32),
            vmem((ROWS, 2 * HEAD), bf16),
            vmem((CHUNKS, PAGES, KEYS), bf16),
            vmem((8, CHUNKS * PAGES), f32),
            vmem((CHUNKS * PAGES, 2 * HEAD), bf16),
            vmem((QROWS, HEAD), bf16),
            vmem((QROWS, HEAD), f32),
            vmem((QROWS, HEAD), f32),
            vmem((QROWS, HEAD), f32),
            vmem((ADAPTERS * RANK2, 2 * HEAD), bf16),
            dma((10,)), dma((NTP,)), dma((NTP,)), dma((2 * NZ,)), dma((2 * NZ,)),
            dma((2 * NZ,)), dma((2 * NZ,)), dma((2 * NZ,)), dma((NTP,)), dma((NTP,)),
        ],
        compiler_params=pltpu.CompilerParams(
            collective_id=0, has_side_effects=True, vmem_limit_bytes=60 << 20
        ),
        name="attention",
    )(
        hidden,
        queries.reshape(ROWS, HEADS * HEAD),
        base.reshape(ROWS, 2 * HEAD),
        adapter.reshape(1, ROWS),
        down,
        up.reshape(ADAPTERS * RANK2, HEAD),
        cache.reshape(SEQ_DEV, CACHE, 2 * HEAD),
        lengths,
        device.reshape(1, ROWS),
        sequence.reshape(1, ROWS),
    )
    return out.reshape(ROWS, 1, HEADS * HEAD)


def solution(mesh):
    return jax.shard_map(
        body,
        mesh=mesh,
        in_specs=(
            P(("group", "ctx"), "tp"),
            P(("group", "ctx"), "tp", None),
            P(("group", "ctx"), "tp", None),
            P(("group", "ctx")),
            P("tp", None),
            P(None, None, None, "tp", None),
            P("ctx", None, "tp", None),
            P("ctx"),
            P("ctx", None),
            P("ctx"),
        ),
        out_specs=P(("group", "ctx"), "tp", None),
        check_vma=False,
    )
```

```python
import math

import jax
import jax.numpy as jnp
from jax import lax
from jax.experimental import pallas as pl
from jax.experimental.pallas import tpu as pltpu
from jax.sharding import PartitionSpec as P

MESH = pl.DeviceIdType.MESH
ROWS = 128
HEADS = 8
HEAD = 128
RANK2 = 128
ADAPTERS = 4
SEQ_DEV = 32
CACHE = 128
IDROWS = 8
NZ = 16
NTP = 8
QROWS = ROWS * HEADS
GROUPS = 8
NEG = -1e30
SCALE = math.log2(math.e) / math.sqrt(HEAD)

ORDER = [0, 1, 15, 3, 13, 2, 14, 4, 12, 6, 10, 5, 11, 7, 9, 8]
PLACE = {slot: i for i, slot in enumerate(ORDER)}
CHUNK = 4
CHUNKS = NZ // CHUNK
KEYS = CHUNK * 2 * ROWS
PAGES = CHUNK * 2 * 8
OWN_SENDS = [(0, 3, 3), (0, -3, 13), (0, 1, 1), (0, -1, 15)]
FORWARDS = {
    3: [(3, 3, 6), (3, 1, 4)],
    13: [(13, -3, 10), (13, -1, 12)],
    1: [(1, 1, 2)],
    15: [(15, -1, 14)],
    4: [(4, 1, 5)],
    12: [(12, -1, 11)],
    6: [(6, 2, 8), (6, 1, 7)],
    10: [(10, -1, 9)],
}
RELAYS = [send for sends in FORWARDS.values() for send in sends]
ARRIVALS = [
    (3, 0), (13, 0), (1, 0), (15, 0), (4, 0), (12, 0), (2, 0), (14, 0), (6, 0), (10, 0), (0, 1),
    (3, 1), (13, 1), (1, 1), (15, 1), (5, 0), (11, 0), (2, 1), (14, 1), (4, 1), (12, 1), (6, 1),
    (10, 1), (7, 0), (9, 0), (8, 0), (5, 1), (11, 1), (7, 1), (9, 1), (8, 1),
]
BOTH = (7, 8, 9)
LAST = 256
PARTIAL_ORDER = (3, 5, 4, 7, 1, 6, 2)


def kernel(
    hid_ref, q_ref, base_ref, idx_ref, down_ref, up_ref, cache_ref, len_ref, rd_ref, rs_ref,
    out_ref,
    hid, qin, base, idx, down, up, cache, lens, rd, rs,
    part, landed, whole, kv, ids, fresh, choose, code_row, handed, q, top, acc, tot, wide,
    load_sem, tp_send, tp_recv, kv_send, kv_recv, core_send, id_send, id_recv,
    share_send, share_recv,
):
    group = lax.axis_index("group")
    ctx = lax.axis_index("ctx")
    tp = lax.axis_index("tp")
    z = ctx // 2
    x_lo = ctx % 2

    def at(step, other, core):
        side = 1 - x_lo if other else x_lo
        return {"group": core, "ctx": lax.rem(z + step + NZ, NZ) * 2 + side}

    barrier = pltpu.get_barrier_semaphore()

    def greet(peers):
        for peer in peers:
            pl.semaphore_signal(barrier, inc=1, device_id=peer, device_id_type=MESH)

    tp_peers = [{"tp": lax.rem(tp + d, NTP)} for d in range(1, NTP)]
    greet(tp_peers)

    @pl.when(group == 0)
    def _():
        greet([at(0, False, 1)])

    @pl.when(group == 1)
    def _():
        greet([at(step, False, 0) for step in (3, -3, 1, -1, 0)] + [at(0, True, 0)])
        greet([at(step, False, 1) for step in (3, -3, 2, -2, 1, -1)] + [at(0, True, 1)])
        greet([at(step, True, 1) for step in (-2, -1, 1)])

    loads = [
        pltpu.make_async_copy(src, dst, load_sem.at[i])
        for i, (src, dst) in enumerate(
            [(hid_ref, hid), (down_ref, down), (idx_ref, idx), (up_ref, up), (base_ref, base),
             (rd_ref, rd), (rs_ref, rs), (q_ref, qin), (len_ref, lens), (cache_ref, cache)]
        )
    ]
    for load in loads[:9]:
        load.start()

    @pl.when(group == 1)
    def _():
        loads[9].start()

    for load in loads[:3]:
        load.wait()

    eye = lax.broadcasted_iota(jnp.int32, (ROWS, ROWS), 0) == lax.broadcasted_iota(
        jnp.int32, (ROWS, ROWS), 1
    )
    adapter = jnp.sum(
        jnp.where(eye, jnp.broadcast_to(idx[...].astype(jnp.float32), (ROWS, ROWS)), 0.0),
        axis=1,
        keepdims=True,
    )
    shrunk = jnp.dot(hid[...], down[...], preferred_element_type=jnp.float32)
    picked = jnp.zeros((ROWS, RANK2), jnp.float32)
    for a in range(ADAPTERS):
        picked = jnp.where(adapter == float(a), shrunk[:, a * RANK2 : (a + 1) * RANK2], picked)
    part[...] = picked

    @pl.when(group == 0)
    def _():
        pl.semaphore_wait(barrier, 13)

    @pl.when(group == 1)
    def _():
        pl.semaphore_wait(barrier, 18)

    tp_copies = [
        pltpu.make_async_remote_copy(
            src_ref=part, dst_ref=landed.at[d],
            send_sem=tp_send.at[d], recv_sem=tp_recv.at[d],
            device_id=tp_peers[d - 1], device_id_type=MESH,
        )
        for d in range(1, NTP)
    ]

    def piece(index):
        return pl.ds(pl.multiple_of(index * 16, 16), 16)

    piece_copies = [
        pltpu.make_async_remote_copy(
            src_ref=part.at[piece(lax.rem(tp + d, NTP))], dst_ref=landed.at[d, :16],
            send_sem=tp_send.at[d], recv_sem=tp_recv.at[d],
            device_id=tp_peers[d - 1], device_id_type=MESH,
        )
        for d in range(1, NTP)
    ]
    share_copies = [
        pltpu.make_async_remote_copy(
            src_ref=whole.at[piece(tp)], dst_ref=whole.at[piece(tp)],
            send_sem=share_send.at[d], recv_sem=share_recv.at[d],
            device_id=tp_peers[d - 1], device_id_type=MESH,
        )
        for d in range(1, NTP)
    ]

    def id_copy(source, step, dest, side):
        i = 2 * dest + side
        return pltpu.make_async_remote_copy(
            src_ref=ids.at[source, 0], dst_ref=ids.at[dest, side],
            send_sem=id_send.at[i], recv_sem=id_recv.at[i],
            device_id=at(step, side == 1, 1), device_id_type=MESH,
        )

    @pl.when(group == 0)
    def _():
        for d in PARTIAL_ORDER:
            tp_copies[d - 1].start()

    for load in loads[3:9]:
        load.wait()

    @pl.when(group == 1)
    def _():
        ids[0, 0] = jnp.concatenate(
            [rd[...], rs[...], jnp.zeros((IDROWS - 2, ROWS), jnp.int32)], axis=0
        )
        for d in PARTIAL_ORDER:
            piece_copies[d - 1].start()
        for send in OWN_SENDS:
            id_copy(*send, 0).start()
        id_copy(0, 0, 0, 1).start()

    for g in range(GROUPS):
        for j in range(HEADS):
            q[g * 128 + j * 16 : g * 128 + (j + 1) * 16, :] = qin[
                g * 16 : (g + 1) * 16, j * HEAD : (j + 1) * HEAD
            ]
    is_key = (lax.broadcasted_iota(jnp.int32, (ADAPTERS * RANK2, HEAD), 0) // 64) % 2 == 0
    up_f = up[...].astype(jnp.float32)
    wide[:, :HEAD] = jnp.where(is_key, up_f, 0.0).astype(jnp.bfloat16)
    wide[:, HEAD:] = jnp.where(is_key, 0.0, up_f).astype(jnp.bfloat16)

    def scores_of(queries, keys):
        return lax.dot_general(
            queries, keys, (((1,), (1,)), ((), ())), preferred_element_type=jnp.float32
        )

    def weighted(weights, values):
        ones = jnp.ones(values.shape, jnp.bfloat16)
        return jnp.dot(
            weights.astype(jnp.bfloat16),
            jnp.concatenate([values, ones], axis=1),
            preferred_element_type=jnp.float32,
        )

    def first_keys(rows, scores, values):
        peak = jnp.max(scores, axis=1, keepdims=True)
        both = weighted(jnp.exp2((scores - peak) * SCALE), values)
        top[rows, :] = jnp.broadcast_to(peak, (peak.shape[0], HEAD))
        acc[rows, :] = both[:, :HEAD]
        tot[rows, :] = both[:, HEAD:]

    def more_keys(rows, scores, values):
        before = top[rows, :]
        after = jnp.maximum(before, jnp.max(scores, axis=1, keepdims=True))
        rescale = jnp.exp2((before - after) * SCALE)
        both = weighted(jnp.exp2((scores - after[:, :1]) * SCALE), values)
        top[rows, :] = after
        acc[rows, :] = acc[rows, :] * rescale + both[:, :HEAD]
        tot[rows, :] = tot[rows, :] * rescale + both[:, HEAD:]

    def emit(group_row, result):
        for g in range(result.shape[0] // 128):
            first = (group_row + g) * 16
            for j in range(HEADS):
                start = g * 128 + j * 16
                out_ref[first : first + 16, j * HEAD : (j + 1) * HEAD] = result[start : start + 16]

    row16 = lax.broadcasted_iota(jnp.int32, (128, 1), 0) % 16

    def own_rows(total):
        spread = jnp.concatenate(
            [
                jnp.where(adapter == float(a), total, 0.0).astype(jnp.bfloat16)
                for a in range(ADAPTERS)
            ],
            axis=1,
        )
        delta = jnp.dot(spread, wide[...], preferred_element_type=jnp.float32)
        return (base[...].astype(jnp.float32) + delta).astype(jnp.bfloat16)

    @pl.when(group == 1)
    def _():
        loads[9].wait()
        column = lax.broadcasted_iota(jnp.int32, (1, CACHE), 1)
        for g in range(GROUPS):
            rows = slice(g * 128, (g + 1) * 128)
            block = cache[4 * g : 4 * g + 4].reshape(4 * CACHE, 2 * HEAD)
            scores = scores_of(q[rows, :], block[:, :HEAD])
            own = row16 // 4
            pieces = []
            for n in range(4):
                ok = jnp.logical_and(own == n, column < lens[4 * g + n])
                pieces.append(jnp.where(ok, scores[:, n * CACHE : (n + 1) * CACHE], NEG))
            first_keys(rows, jnp.concatenate(pieces, axis=1), block[:, HEAD:])

        summed = part[piece(tp), :]
        for d in range(1, NTP):
            piece_copies[d - 1].wait_recv()
            summed = summed + landed[d, :16]
        whole[piece(tp), :] = summed.astype(jnp.bfloat16)
        for d in PARTIAL_ORDER:
            share_copies[d - 1].start()
        for slot, side in ARRIVALS:
            if side == 0:
                id_copy(0, 1, slot, 0).wait_recv()
                for send in FORWARDS.get(slot, []):
                    id_copy(*send, 0).start()
                id_copy(slot, 0, slot, 1).start()
            else:
                id_copy(slot, 0, slot, 1).wait_recv()
            if (slot, side) == (5, 1):
                for copy in share_copies:
                    copy.wait_recv()
                fresh[...] = own_rows(whole[...].astype(jnp.float32))
        page = lax.broadcasted_iota(jnp.int32, (PAGES, KEYS), 0)
        key = lax.broadcasted_iota(jnp.int32, (PAGES, KEYS), 1)
        same = jnp.logical_and(page // 8 == key // ROWS, page % 8 == key % 8)
        spread8 = lax.broadcasted_iota(
            jnp.int32, (2 * CHUNK, PAGES), 0
        ) == lax.broadcasted_iota(jnp.int32, (2 * CHUNK, PAGES), 1) // 8
        codes = []
        for c in range(CHUNKS):
            slots = ORDER[c * CHUNK : (c + 1) * CHUNK]
            device = jnp.concatenate([ids[s, d, :1] for s in slots for d in (0, 1)], axis=1)
            mine = jnp.logical_and(same, device == ctx)
            choose[c] = jnp.where(mine, 1.0, 0.0).astype(jnp.bfloat16)
            device = jnp.concatenate([ids[s, d, :1] for s in slots for d in (0, 1)], axis=0)
            sequence = jnp.concatenate([ids[s, d, 1:2] for s in slots for d in (0, 1)], axis=0)
            sequence = jnp.where(device == ctx, sequence, -1).astype(jnp.float32)
            sequence = jnp.max(sequence, axis=1, keepdims=True)
            codes.append(jnp.sum(jnp.where(spread8, sequence, 0.0), axis=0, keepdims=True))
        code_row[...] = jnp.broadcast_to(jnp.concatenate(codes, axis=1), code_row.shape)

    def kv_copy(source, step, dest, side):
        i = 2 * PLACE[dest] + side
        return pltpu.make_async_remote_copy(
            src_ref=kv.at[PLACE[source], 0], dst_ref=kv.at[PLACE[dest], side],
            send_sem=kv_send.at[i], recv_sem=kv_recv.at[i],
            device_id=at(step, side == 1, 1), device_id_type=MESH,
        )

    def core_copy(slot, side):
        i = 2 * PLACE[slot] + side
        return pltpu.make_async_remote_copy(
            src_ref=kv.at[PLACE[slot], side], dst_ref=kv.at[PLACE[slot], side],
            send_sem=core_send.at[i], recv_sem=kv_recv.at[i],
            device_id={"group": 1 - group}, device_id_type=MESH,
        )

    def chunk_of(c):
        block = kv[c * CHUNK : (c + 1) * CHUNK].reshape(KEYS, 2 * HEAD)
        return block[:, :HEAD], block[:, HEAD:]

    @pl.when(group == 0)
    def _():
        total = picked
        for d in range(1, NTP):
            tp_copies[d - 1].wait_recv()
            total = total + landed[d]
        kv[0, 0] = own_rows(total)
        for send in OWN_SENDS:
            kv_copy(*send, 0).start()
        kv_copy(0, 0, 0, 1).start()
        core_copy(0, 0).start()
        for c in range(CHUNKS):
            slots = ORDER[c * CHUNK : (c + 1) * CHUNK]
            for slot in slots:
                for side in (0, 1):
                    if (slot, side) != (0, 0):
                        core_copy(slot, side).wait_recv()
            limit = [jnp.where(z >= slot, 0.0, NEG) for slot in slots for _ in (0, 1)]
            if c == 0:
                limit[1] = jnp.where(x_lo == 1, 0.0, NEG)

            def chunk(c=c, slots=slots, limit=limit):
                keys, values = chunk_of(c)
                bias = jnp.concatenate(
                    [jnp.full((1, ROWS), value, jnp.float32) for value in limit], axis=1
                )
                for g in range(GROUPS):
                    rows = slice(g * 128, (g + 1) * 128)
                    scores = scores_of(q[rows, :], keys) + bias
                    if c == 0:
                        column = lax.broadcasted_iota(jnp.int32, (1, ROWS), 1)
                        diagonal = jnp.where(column <= g * 16 + row16, scores[:, :ROWS], NEG)
                        scores = jnp.concatenate([diagonal, scores[:, ROWS:]], axis=1)
                        first_keys(rows, scores, values)
                    else:
                        more_keys(rows, scores, values)

            if c == 0:
                chunk()
            else:
                pl.when(z >= min(slots))(chunk)

    @pl.when(group == 1)
    def _():
        seen = set()
        seen.add((0, 0))
        ready = 0
        for slot, side in ARRIVALS:
            if side == 0:
                kv_copy(0, 1, slot, 0).wait_recv()
                for send in FORWARDS.get(slot, []):
                    kv_copy(*send, 0).start()
                    if send[2] in BOTH:
                        kv_copy(*send, 1).start()
                if slot not in BOTH:
                    kv_copy(slot, 0, slot, 1).start()
            else:
                kv_copy(slot, 0, slot, 1).wait_recv()
            core_copy(slot, side).start()
            seen.add((slot, side))
            if (slot, side) == (0, 1):
                core_copy(0, 0).wait_recv()
            slots = ORDER[ready * CHUNK : (ready + 1) * CHUNK]
            if all((s, d) in seen for s in slots for d in (0, 1)):
                block = kv[ready * CHUNK : (ready + 1) * CHUNK].reshape(KEYS, 2 * HEAD)
                handed[ready * PAGES : (ready + 1) * PAGES, :] = jnp.dot(
                    choose[ready], block, preferred_element_type=jnp.float32
                ).astype(jnp.bfloat16)
                ready += 1
        assert ready == CHUNKS
        code = code_row[:1, :]
        both = jnp.concatenate([handed[...], fresh[...]], axis=0)
        column = lax.broadcasted_iota(jnp.int32, (1, ROWS), 1)
        row = lax.broadcasted_iota(jnp.int32, (LAST, 1), 0)
        for i in range(QROWS // LAST):
            rows = slice(i * LAST, (i + 1) * LAST)
            token = (i * (LAST // 128) + row // 128) * 16 + row % 16
            scores = scores_of(q[rows, :], both[:, :HEAD])
            step_ok = jnp.logical_and(column // 4 == token // 4, column <= token)
            handed_ok = code == (token // 4).astype(jnp.float32)
            scores = jnp.concatenate(
                [
                    jnp.where(handed_ok, scores[:, : CHUNKS * PAGES], NEG),
                    jnp.where(step_ok, scores[:, CHUNKS * PAGES :], NEG),
                ],
                axis=1,
            )
            before = top[rows, :]
            after = jnp.maximum(before, jnp.max(scores, axis=1, keepdims=True))
            rescale = jnp.exp2((before - after) * SCALE)
            sums = weighted(jnp.exp2((scores - after[:, :1]) * SCALE), both[:, HEAD:])
            total = tot[rows, :] * rescale + sums[:, HEAD:]
            result = (acc[rows, :] * rescale + sums[:, :HEAD]) / total
            emit(i * (LAST // 128), result.astype(jnp.bfloat16))

    @pl.when(group == 0)
    def _():
        for g in range(GROUPS):
            rows = slice(g * 128, (g + 1) * 128)
            emit(g, (acc[rows, :] / tot[rows, :]).astype(jnp.bfloat16))

    @pl.when(group == 0)
    def _():
        for copy in tp_copies:
            copy.wait_send()
        for send in OWN_SENDS:
            kv_copy(*send, 0).wait_send()
        kv_copy(0, 0, 0, 1).wait_send()
        core_copy(0, 0).wait_send()

    @pl.when(group == 1)
    def _():
        for copy in piece_copies + share_copies:
            copy.wait_send()
        for send in OWN_SENDS:
            id_copy(*send, 0).wait_send()
        id_copy(0, 0, 0, 1).wait_send()
        for send in RELAYS:
            id_copy(*send, 0).wait_send()
            kv_copy(*send, 0).wait_send()
            if send[2] in BOTH:
                kv_copy(*send, 1).wait_send()
        for slot, side in ARRIVALS:
            core_copy(slot, side).wait_send()
            if side == 0:
                id_copy(slot, 0, slot, 1).wait_send()
                if slot not in BOTH:
                    kv_copy(slot, 0, slot, 1).wait_send()


def body(hidden, queries, base, adapter, down, up, cache, lengths, device, sequence):
    vmem = pltpu.VMEM
    dma = pltpu.SemaphoreType.DMA
    bf16, f32, i32 = jnp.bfloat16, jnp.float32, jnp.int32
    out = pl.pallas_call(
        kernel,
        out_shape=jax.ShapeDtypeStruct((ROWS, HEADS * HEAD), bf16),
        in_specs=[pl.BlockSpec(memory_space=pl.ANY)] * 10,
        out_specs=pl.BlockSpec(memory_space=vmem),
        scratch_shapes=[
            vmem((ROWS, 1024), bf16),
            vmem((ROWS, HEADS * HEAD), bf16),
            vmem((ROWS, 2 * HEAD), bf16),
            vmem((1, ROWS), i32),
            vmem((1024, ADAPTERS * RANK2), bf16),
            vmem((ADAPTERS * RANK2, HEAD), bf16),
            vmem((SEQ_DEV, CACHE, 2 * HEAD), bf16),
            pltpu.SMEM((SEQ_DEV,), i32),
            vmem((1, ROWS), i32),
            vmem((1, ROWS), i32),
            vmem((ROWS, RANK2), f32),
            vmem((NTP, ROWS, RANK2), f32),
            vmem((ROWS, RANK2), bf16),
            vmem((NZ, 2, ROWS, 2 * HEAD), bf16),
            vmem((NZ, 2, IDROWS, ROWS), i32),
            vmem((ROWS, 2 * HEAD), bf16),
            vmem((CHUNKS, PAGES, KEYS), bf16),
            vmem((8, CHUNKS * PAGES), f32),
            vmem((CHUNKS * PAGES, 2 * HEAD), bf16),
            vmem((QROWS, HEAD), bf16),
            vmem((QROWS, HEAD), f32),
            vmem((QROWS, HEAD), f32),
            vmem((QROWS, HEAD), f32),
            vmem((ADAPTERS * RANK2, 2 * HEAD), bf16),
            dma((10,)), dma((NTP,)), dma((NTP,)), dma((2 * NZ,)), dma((2 * NZ,)),
            dma((2 * NZ,)), dma((2 * NZ,)), dma((2 * NZ,)), dma((NTP,)), dma((NTP,)),
        ],
        compiler_params=pltpu.CompilerParams(
            collective_id=0, has_side_effects=True, vmem_limit_bytes=60 << 20
        ),
        name="attention",
    )(
        hidden,
        queries.reshape(ROWS, HEADS * HEAD),
        base.reshape(ROWS, 2 * HEAD),
        adapter.reshape(1, ROWS),
        down,
        up.reshape(ADAPTERS * RANK2, HEAD),
        cache.reshape(SEQ_DEV, CACHE, 2 * HEAD),
        lengths,
        device.reshape(1, ROWS),
        sequence.reshape(1, ROWS),
    )
    return out.reshape(ROWS, 1, HEADS * HEAD)


def solution(mesh):
    return jax.shard_map(
        body,
        mesh=mesh,
        in_specs=(
            P(("group", "ctx"), "tp"),
            P(("group", "ctx"), "tp", None),
            P(("group", "ctx"), "tp", None),
            P(("group", "ctx")),
            P("tp", None),
            P(None, None, None, "tp", None),
            P("ctx", None, "tp", None),
            P("ctx"),
            P("ctx", None),
            P("ctx"),
        ),
        out_specs=P(("group", "ctx"), "tp", None),
        check_vma=False,
    )
```
